256 devices in a mesh: row: 8 (over y_lo, x), col: 32 (over y_hi, z, core).
Axes of the slice: x: 4, y: 4 (y_hi: 2, y_lo: 2; y = y_hi * 2 + y_lo), z: 8, core: 2. Of those that a mesh axis runs over, the one named last changes fastest.
Arguments:
- queries: bfloat16 [24576, 1024], P(('row', 'col')), may hold values from -128 to 128
- keys: bfloat16 [24576, 128], P(('row', 'col')), may hold values from -4 to 4
- values: bfloat16 [24576, 128], P(('row', 'col')), may hold values from -6 to 6
- block_start: int32 [256], P(('row', 'col')), may hold values from 0 to 255, as said below
Outputs:
- attended: float32 [24576, 1024], P(('row', 'col'))
- log_total: float32 [24576, 8], P(('row', 'col'))
The draws below stay inside these ranges and needn't reach their ends.
Inputs may be any that keep to these rules, and one draw needn't show every extreme that they name: `block_start`: a permutation of 0 to 255.
All inputs are finite; a program needn't handle non-finite values.
Results may differ from the reference program's by a relative error of at most 0.0028.
Values may be sent and summed in bfloat16 or wider, within the bound.
A program may use at most 64 MiB of HBM per device.

```python
import jax
import jax.numpy as jnp
from jax import lax

HD = 128
QH = 8
TOK_DEV = 96
BLOCKS = 256
TOKENS = 24576


def shared_keys(key):
    return jnp.clip(jax.random.normal(jax.random.fold_in(key, 11), (TOKENS, HD), jnp.float32), -4.0, 4.0)


def draw_keys(key, part):
    return shared_keys(key).astype(jnp.bfloat16)


def draw_block_start(key, part):
    return jax.random.permutation(jax.random.fold_in(key, 13), BLOCKS).astype(jnp.int32)


def draw_queries(key, part):
    sub_key = jax.random.fold_in(key, 12)
    result = jnp.clip(3.0 * jax.random.normal(sub_key, (TOKENS, QH * HD), jnp.float32), -12.0, 12.0)
    return result.astype(jnp.bfloat16)


def level_of(own_key, extent, pieces, least, largest):
    def one(dim, blocks):
        draws = jax.random.uniform(jax.random.fold_in(jax.random.fold_in(own_key, 6), dim), (blocks,), jnp.float32, least / len(pieces), largest / len(pieces))
        return jnp.repeat(jnp.exp(draws), extent[dim] // blocks).reshape((-1,) + (1,) * (len(extent) - dim - 1))

    factor_of = one(*pieces[0])
    for cut in pieces[1:]:
        factor_of = factor_of * one(*cut)
    return factor_of


def scatter_about(stream_key, shape, deviation, reach, cuts=(), kind=jnp.bfloat16):
    factor_of = level_of(stream_key, shape, cuts, -0.22, 0.18) if cuts else 1.0
    values = jax.random.normal(stream_key, shape, jnp.float32) * deviation * factor_of
    return jnp.minimum(jnp.maximum(values, -reach), reach).astype(kind)


def setup_inputs(seed: int = 0) -> dict:
    streams_of = jax.random.split(jax.random.key(seed), 5)
    return {
        "queries": draw_queries(jax.random.fold_in(streams_of[4], 71), 0),
        "keys": draw_keys(jax.random.fold_in(streams_of[4], 71), 0),
        "values": scatter_about(streams_of[2], (TOKENS, HD), 1.0, 6.0, ((0, 256),)),
        "block_start": draw_block_start(jax.random.fold_in(streams_of[4], 71), 0),
    }


def reference(queries, keys, values, block_start):
    scale = HD ** -0.5
    offsets = jnp.arange(TOK_DEV, dtype=jnp.int32)
    positions = (block_start[:, None] * TOK_DEV + offsets[None, :]).reshape(-1).astype(jnp.int32)
    query_blocks = queries.reshape(BLOCKS, TOK_DEV * QH, HD)

    def one_block(items):
        query_rows, begin_at = items
        row_pos = jnp.repeat(begin_at * TOK_DEV + offsets, QH)
        scores = jnp.dot(query_rows, keys.T, preferred_element_type=jnp.float32) * scale
        kept = positions[None, :] <= row_pos[:, None]
        scores = jnp.where(kept, scores, -1e30)
        peak = jnp.max(scores, axis=1)
        weights = jnp.where(kept, jnp.exp(scores - peak[:, None]), 0.0)
        total = jnp.sum(weights, axis=1)
        mixed = jnp.dot(weights.astype(jnp.bfloat16), values, preferred_element_type=jnp.float32)
        result = mixed / total[:, None]
        return result.reshape(TOK_DEV, QH * HD), (peak + jnp.log(total)).reshape(TOK_DEV, QH)

    attended, log_total = lax.map(one_block, (query_blocks, block_start))
    return attended.reshape(TOKENS, QH * HD), log_total.reshape(TOKENS, QH)
```

```python
import functools
import math

import jax
import jax.numpy as jnp
from jax import lax
from jax.experimental import pallas as pl
from jax.experimental.pallas import tpu as pltpu
from jax.sharding import PartitionSpec as P

MESH = pl.DeviceIdType.MESH
TOK = 96
HD = 128
HALF = 4 * TOK
MSG = 2 * TOK + 16
QMSG = HALF + 16
OMSG = HALF + TOK
ROWS = 2 * HALF
KEYS = 8 * TOK
REL = (0, 1, 3, 2)
INV = (0, 2, 1, 3)
GROUPS = ((0, 1), (1, 2), (3, 1))
SCALE = HD ** -0.5
C2 = SCALE * math.log2(math.e)
MASKED = -1e30
FLOOR = -1e20


def kernel(start_ref, q_ref, k_ref, v_ref, att_ref, lt_ref, kv, qb, qother, ob, rb, acc, peak,
           s_a, s_b, p_a, p_b, f_a, f_b,
           y_s, y_r, own_s, own_r, z_s, z_r, hand_s, hand_r, handy_s, handy_r, q_s, q_r, o_s, o_r):
    row = lax.axis_index("row")
    col = lax.axis_index("col")
    x = lax.rem(row, 4)
    y = lax.div(col, 16) * 2 + lax.div(row, 4)
    z = lax.rem(lax.div(col, 2), 8)
    c = lax.rem(col, 2)

    def device(xx, yy, zz, cc):
        return (lax.rem(yy, 2) * 4 + xx, (lax.div(yy, 2) * 8 + zz) * 2 + cc)

    partner = device(x, y, z, 1 - c)
    y_peer = [None] + [device(x, lax.rem(y + REL[k], 4), z, c) for k in (1, 2, 3)]
    z_up = device(x, y, lax.rem(z + 1, 8), c)
    z_down = device(x, y, lax.rem(z + 7, 8), c)
    x_peer = [[None, partner]] + [
        [device(lax.rem(x + REL[k], 4), y, z, c), device(lax.rem(x + REL[k], 4), y, z, 1 - c)]
        for k in (1, 2, 3)
    ]

    barrier = pltpu.get_barrier_semaphore()
    peers = [partner, z_up, z_down] + y_peer[1:] + x_peer[1] + x_peer[2] + x_peer[3]
    for peer in peers:
        pl.semaphore_signal(barrier, inc=1, device_id=peer, device_id_type=MESH)

    number = jnp.full((16, HD), start_ref[0].astype(jnp.float32), jnp.float32).astype(jnp.bfloat16)
    kv[0, 0, 0:TOK, :] = k_ref[...]
    kv[0, 0, TOK:2 * TOK, :] = v_ref[...]
    kv[0, 0, 2 * TOK:MSG, :] = number
    for h in range(4):
        here = pl.ds(pl.multiple_of((c * 4 + h) * HD, HD), HD)
        there = pl.ds(pl.multiple_of(((1 - c) * 4 + h) * HD, HD), HD)
        qb[0, 0, h * TOK:(h + 1) * TOK, :] = q_ref[:, here]
        qother[h * TOK:(h + 1) * TOK, :] = q_ref[:, there]
    qb[0, 0, HALF:QMSG, :] = number
    qother[HALF:QMSG, :] = number
    acc[...] = jnp.zeros_like(acc)
    peak[...] = jnp.full(peak.shape, FLOOR, jnp.float32)

    def copy(src, dst, send, recv, to):
        return pltpu.make_async_remote_copy(
            src_ref=src, dst_ref=dst, send_sem=send, recv_sem=recv, device_id=to, device_id_type=MESH
        )

    sent = []

    def start(make, *which):
        make(*which).start()
        sent.append((make, which))

    def q_copy(k, other):
        if other:
            return copy(qother, qb.at[INV[k], 1], q_s.at[k, 1], q_r.at[INV[k], 1], x_peer[k][1])
        return copy(qb.at[0, 0], qb.at[INV[k], 0], q_s.at[k, 0], q_r.at[INV[k], 0], x_peer[k][0])

    def q_wait(k, other):
        copy(qb.at[k, other], qb.at[k, other], q_s.at[k, other], q_r.at[k, other], partner).wait_recv()

    def y_copy(k):
        return copy(kv.at[0, 0], kv.at[0, INV[k]], y_s.at[k], y_r.at[INV[k]], y_peer[k])

    def y_wait(k):
        copy(kv.at[0, k], kv.at[0, k], y_s.at[k], y_r.at[k], partner).wait_recv()

    def part(slot, g):
        return kv.at[slot, pl.ds(GROUPS[g][0], GROUPS[g][1])]

    def z_copy(slot, g):
        src = 0 if slot <= 2 else slot - 2
        to = z_up if slot % 2 == 1 else z_down
        return copy(part(src, g), part(slot, g), z_s.at[slot, g], z_r.at[slot, g], to)

    def opposite_copy(g):
        to = device(x, y, lax.rem(z + 1 + 6 * c, 8), c)
        return copy(part(5 + c, g), part(7, g), z_s.at[7, g], z_r.at[7, g], to)

    def z_wait(slot, g):
        copy(part(slot, g), part(slot, g), z_s.at[slot, g], z_r.at[slot, g], partner).wait_recv()

    def hand_copy(slot, g):
        dst = kv.at[slot, pl.ds(4 + GROUPS[g][0], GROUPS[g][1])]
        return copy(part(slot, g), dst, hand_s.at[slot, g], hand_r.at[slot, g], partner)

    def hand_wait(slot):
        for g in range(3):
            dst = kv.at[slot, pl.ds(4 + GROUPS[g][0], GROUPS[g][1])]
            copy(dst, dst, hand_s.at[slot, g], hand_r.at[slot, g], partner).wait_recv()

    def arrive(slots, g):
        for slot in slots:
            z_wait(slot, g)
            if slot + 2 <= 6:
                start(z_copy, slot + 2, g)
            start(hand_copy, slot, g)
        if 5 in slots:
            start(opposite_copy, g)

    def own_copy():
        return copy(kv.at[0, 0], kv.at[0, 4], own_s, own_r, partner)

    def row_copy():
        return copy(kv.at[0, pl.ds(1, 3)], kv.at[0, pl.ds(5, 3)], handy_s, handy_r, partner)

    def o_copy(k, other):
        return copy(ob.at[k, other], rb.at[INV[k], other], o_s.at[k, other], o_r.at[INV[k], other], x_peer[k][other])

    def o_wait(k, other):
        copy(rb.at[k, other], rb.at[k, other], o_s.at[k, other], o_r.at[k, other], partner).wait_recv()

    def unit(u):
        if isinstance(u, int):
            a, b = divmod(u + 2, 3)
            if u < 4:
                return u, 0
            if u < 16:
                return b + 1, a - 1
            if u < 25:
                return 9 - a, 5 + b
            return 0, u - 24
        a, b = lax.div(u + 2, 3), lax.rem(u + 2, 3)
        from4, from16, from25 = lax.div(u + 28, 32), lax.div(u + 16, 32), lax.div(u + 7, 32)
        query = (1 - from4) * u + (from4 - from16) * (b + 1) + (from16 - from25) * (9 - a)
        slot = (from4 - from16) * (a - 1) + (from16 - from25) * (5 + b) + from25 * (u - 24)
        return query, slot

    lane = lax.broadcasted_iota(jnp.int32, (1, HD), 1)
    ones = jnp.ones((KEYS, HD), jnp.bfloat16)

    def scores(u, s):
        query, slot = unit(u)
        rows = qb[query, :, 0:HALF, :].reshape(ROWS, HD)
        keys = kv[slot, :, 0:TOK, :].reshape(KEYS, HD)
        s[...] = lax.dot_general(rows, keys, (((1,), (1,)), ((), ())), preferred_element_type=jnp.float32)

    def soften(u, s, p, f, diagonal=False):
        query, slot = unit(u)
        numbers = [kv[slot, i, 2 * TOK:MSG, :].astype(jnp.float32)[0:1, :] for i in range(8)]
        tiles = []
        for t in range(KEYS // HD):
            first = t * HD // TOK
            edge = (first + 1) * TOK - t * HD
            tiles.append(jnp.where(lane < edge, numbers[first], numbers[first + 1]))
        blocks = jnp.concatenate(tiles, axis=1)
        for half in range(2):
            at = pl.ds(half * HALF, HALF)
            mine = qb[query, half, HALF:QMSG, :].astype(jnp.float32)[0:1, :]
            mine = jnp.concatenate([mine] * (KEYS // HD), axis=1)
            v = s[at, :] + jnp.where(blocks > mine, MASKED, 0.0)
            if diagonal:
                key = lax.broadcasted_iota(jnp.int32, (HALF, KEYS), 1)
                token = lax.rem(lax.broadcasted_iota(jnp.int32, (HALF, KEYS), 0), TOK)
                begin = half * 4 * TOK
                later = (key >= begin) & (key < begin + TOK) & (key - begin > token)
                v = jnp.where(later, MASKED, v)
            old = peak[query, at, :]
            new = jnp.maximum(old, jnp.max(v, axis=1, keepdims=True))
            p[at, :] = jnp.exp2((v - new[:, :1]) * C2).astype(jnp.bfloat16)
            f[at, :] = jnp.exp2((old - new) * C2)
            peak[query, at, :] = new

    def gather(u, p, f):
        query, slot = unit(u)
        vals = kv[slot, :, TOK:2 * TOK, :].reshape(KEYS, HD)
        vals = jnp.concatenate([vals, ones], axis=1)
        factor = jnp.concatenate([f[...], f[...]], axis=1)
        acc[query] = acc[query] * factor + jnp.dot(p[...], vals, preferred_element_type=jnp.float32)

    def finish(k):
        for half in range(2):
            at = pl.ds(half * HALF, HALF)
            total = acc[k, at, HD:2 * HD]
            some = total > 0.0
            safe = jnp.where(some, total, 1.0)
            ob[k, half, 0:HALF, :] = (acc[k, at, 0:HD] / safe).astype(jnp.bfloat16)
            log = jnp.where(some, peak[k, at, :] * SCALE + jnp.log(safe), MASKED)
            hi = log.astype(jnp.bfloat16).astype(jnp.float32)
            mid = (log - hi).astype(jnp.bfloat16).astype(jnp.float32)
            low = log - hi - mid
            packed = jnp.zeros((TOK, HD), jnp.float32)
            for h in range(4):
                for i, term in enumerate((hi, mid, low)):
                    packed = jnp.where(lane == 3 * h + i, term[h * TOK:(h + 1) * TOK, :], packed)
            ob[k, half, HALF:OMSG, :] = packed.astype(jnp.bfloat16)

    def send_out(k):
        finish(k)
        for other in range(2):
            if k or other:
                start(o_copy, k, other)

    pl.semaphore_wait(barrier, len(peers))
    start(q_copy, 0, 1)
    start(own_copy)
    for k in (1, 2, 3):
        start(y_copy, k)
        if k < 3:
            start(z_copy, k, 0)
        for other in range(2):
            start(q_copy, k, other)
    for k in (1, 2):
        y_wait(k)
    start(z_copy, 1, 1)
    start(z_copy, 2, 1)
    y_wait(3)
    start(z_copy, 1, 2)
    start(z_copy, 2, 2)
    start(row_copy)
    own_copy().wait_recv()
    q_wait(0, 1)
    arrive((1, 2), 0)
    row_copy().wait_recv()
    scores(0, s_a)
    q_wait(1, 0)
    q_wait(1, 1)
    scores(1, s_b)
    soften(0, s_a, p_a, f_a, diagonal=True)

    def events(t):
        def at(step):
            return pl.when(t == step)

        @at(0)
        def _():
            for k in (2, 3):
                q_wait(k, 0)
                q_wait(k, 1)

        @at(1)
        def _():
            arrive((1, 2), 1)
            arrive((3, 4), 0)
            arrive((1, 2), 2)
            hand_wait(1)
            hand_wait(2)

        @at(3)
        def _():
            arrive((3, 4), 1)
            arrive((5, 6), 0)

        @at(4)
        def _():
            arrive((3, 4), 2)
            hand_wait(3)
            hand_wait(4)

        @at(6)
        def _():
            arrive((5, 6), 1)
            arrive((5, 6), 2)

        @at(7)
        def _():
            hand_wait(5)
            hand_wait(6)

        @at(8)
        def _():
            for g in range(3):
                z_wait(7, g)
                start(hand_copy, 7, g)
            hand_wait(7)

        @at(11)
        def _():
            send_out(3)

        @at(12)
        def _():
            send_out(2)

        @at(14)
        def _():
            send_out(1)

    def turn(t, carry):
        events(t)
        i = 2 * t + 1
        scores(i + 1, s_a)
        soften(i, s_b, p_b, f_b)
        gather(i - 1, p_a, f_a)
        scores(i + 2, s_b)
        soften(i + 1, s_a, p_a, f_a)
        gather(i, p_b, f_b)
        return carry

    lax.fori_loop(0, 15, turn, 0)
    soften(31, s_b, p_b, f_b)
    gather(30, p_a, f_a)
    gather(31, p_b, f_b)
    send_out(0)

    for make, which in sent:
        make(*which).wait_send()
    for k in range(4):
        for other in range(2):
            if k or other:
                o_wait(k, other)

    totals = jnp.zeros((TOK, HD), jnp.float32)
    for other in range(2):
        half = c if other == 0 else 1 - c
        parts = [ob.at[0, 0] if k == 0 and other == 0 else rb.at[k, other] for k in range(4)]
        logs = [part_ref[HALF:OMSG, :].astype(jnp.float32) for part_ref in parts]
        for h in range(4):
            log = [v[:, 3 * h:3 * h + 1] + v[:, 3 * h + 1:3 * h + 2] + v[:, 3 * h + 2:3 * h + 3] for v in logs]
            most = jnp.maximum(jnp.maximum(log[0], log[1]), jnp.maximum(log[2], log[3]))
            share = [jnp.exp(v - most) for v in log]
            whole = share[0] + share[1] + share[2] + share[3]
            mixed = jnp.zeros((TOK, HD), jnp.float32)
            for k in range(4):
                mixed += (share[k] / whole) * parts[k][h * TOK:(h + 1) * TOK, :].astype(jnp.float32)
            att_ref[:, pl.ds(pl.multiple_of((half * 4 + h) * HD, HD), HD)] = mixed
            totals = jnp.where(lane == half * 4 + h, most + jnp.log(whole), totals)
    lt_ref[...] = totals[:, 0:8]


def local(queries, keys, values, block_start):
    vmem = pl.BlockSpec(memory_space=pltpu.VMEM)
    dma = pltpu.SemaphoreType.DMA
    bf16, f32 = jnp.bfloat16, jnp.float32
    return pl.pallas_call(
        kernel,
        out_shape=(
            jax.ShapeDtypeStruct((TOK, 8 * HD), f32),
            jax.ShapeDtypeStruct((TOK, 8), f32),
        ),
        in_specs=[pl.BlockSpec(memory_space=pltpu.SMEM), vmem, vmem, vmem],
        out_specs=(vmem, vmem),
        scratch_shapes=[
            pltpu.VMEM((8, 8, MSG, HD), bf16),
            pltpu.VMEM((4, 2, QMSG, HD), bf16),
            pltpu.VMEM((QMSG, HD), bf16),
            pltpu.VMEM((4, 2, OMSG, HD), bf16),
            pltpu.VMEM((4, 2, OMSG, HD), bf16),
            pltpu.VMEM((4, ROWS, 2 * HD), f32),
            pltpu.VMEM((4, ROWS, HD), f32),
            pltpu.VMEM((ROWS, KEYS), f32),
            pltpu.VMEM((ROWS, KEYS), f32),
            pltpu.VMEM((ROWS, KEYS), bf16),
            pltpu.VMEM((ROWS, KEYS), bf16),
            pltpu.VMEM((ROWS, HD), f32),
            pltpu.VMEM((ROWS, HD), f32),
            dma((4,)), dma((4,)), dma, dma, dma((8, 3)), dma((8, 3)), dma((8, 3)), dma((8, 3)), dma, dma,
            dma((4, 2)), dma((4, 2)), dma((4, 2)), dma((4, 2)),
        ],
        compiler_params=pltpu.CompilerParams(
            collective_id=0, has_side_effects=True, vmem_limit_bytes=48 << 20
        ),
    )(block_start, queries, keys, values)


def solution(mesh):
    placed = (
        P(("row", "col"), None),
        P(("row", "col"), None),
        P(("row", "col"), None),
        P(("row", "col")),
    )
    return jax.shard_map(
        local,
        mesh=mesh,
        in_specs=placed,
        out_specs=(P(("row", "col"), None), P(("row", "col"), None)),
        check_vma=False,
    )
```

```python
import functools
import math

import jax
import jax.numpy as jnp
from jax import lax
from jax.experimental import pallas as pl
from jax.experimental.pallas import tpu as pltpu
from jax.sharding import PartitionSpec as P

MESH = pl.DeviceIdType.MESH
TOK = 96
HD = 128
HALF = 4 * TOK
MSG = 2 * TOK + 16
QMSG = HALF + 16
OMSG = HALF + TOK
ROWS = 2 * HALF
KEYS = 8 * TOK
REL = (0, 1, 3, 2)
INV = (0, 2, 1, 3)
Z_OFF = (0, 1, 7, 2, 6, 3, 5, 4)
Z_INV = (0, 2, 1, 4, 3, 6, 5, 7)
PLANE_AT = (1, 1, 2, 2, 5, 5, 7, 7)
LINE_AT = (0, 3, 4, 6)
SCALE = HD ** -0.5
C2 = SCALE * math.log2(math.e)
MASKED = -1e30
FLOOR = -1e20


def kernel(start_ref, q_hbm, k_hbm, v_hbm, att_ref, lt_ref, q_ref, kv, qb, qother, ob, rb, acc, peak,
           marks, triangle, s_a, s_b, p_a, p_b, f_a, f_b,
           y_s, y_r, z_s, z_r, a_s, a_r, b_s, b_r, ah_s, bh_s, q_s, q_r, o_s, o_r, in_s):
    row = lax.axis_index("row")
    col = lax.axis_index("col")
    x = lax.rem(row, 4)
    y = lax.div(col, 16) * 2 + lax.div(row, 4)
    z = lax.rem(lax.div(col, 2), 8)
    c = lax.rem(col, 2)

    def device(xx, yy, zz, cc):
        return (lax.rem(yy, 2) * 4 + xx, (lax.div(yy, 2) * 8 + zz) * 2 + cc)

    partner = device(x, y, z, 1 - c)
    y_peer = [None] + [device(x, lax.rem(y + REL[k], 4), z, c) for k in (1, 2, 3)]
    z_up = device(x, y, lax.rem(z + 1, 8), c)
    z_down = device(x, y, lax.rem(z + 7, 8), c)
    z_peer = [device(x, y, lax.rem(z + step, 8), c) for step in Z_OFF]
    x_peer = [[None, partner]] + [
        [device(lax.rem(x + REL[k], 4), y, z, c), device(lax.rem(x + REL[k], 4), y, z, 1 - c)]
        for k in (1, 2, 3)
    ]

    barrier = pltpu.get_barrier_semaphore()

    def greet(peers):
        for peer in peers:
            pl.semaphore_signal(barrier, inc=1, device_id=peer, device_id_type=MESH)

    greet([partner, z_up, z_down, y_peer[1], y_peer[2]] + x_peer[1] + x_peer[2] + x_peer[3])

    @pl.when(c == 0)
    def _():
        greet([y_peer[3]])

    @pl.when(c == 1)
    def _():
        greet(z_peer[3:])

    loads = [
        pltpu.make_async_copy(k_hbm, kv.at[1 - c, 0, pl.ds(0, TOK)], in_s.at[0]),
        pltpu.make_async_copy(v_hbm, kv.at[1 - c, 0, pl.ds(TOK, TOK)], in_s.at[1]),
        pltpu.make_async_copy(q_hbm, q_ref, in_s.at[2]),
    ]
    for load in loads:
        load.start()
    acc[...] = jnp.zeros_like(acc)
    peak[...] = jnp.full(peak.shape, FLOOR, jnp.float32)

    number = jnp.full((16, HD), start_ref[0].astype(jnp.float32), jnp.float32).astype(jnp.bfloat16)
    kv[1 - c, 0, 2 * TOK:MSG, :] = number
    for load in loads:
        load.wait()
    for h in range(4):
        here = pl.ds(pl.multiple_of((c * 4 + h) * HD, HD), HD)
        there = pl.ds(pl.multiple_of(((1 - c) * 4 + h) * HD, HD), HD)
        qb[0, 0, h * TOK:(h + 1) * TOK, :] = q_ref[:, here]
        qother[h * TOK:(h + 1) * TOK, :] = q_ref[:, there]
    qb[0, 0, HALF:QMSG, :] = number
    qother[HALF:QMSG, :] = number

    def copy(src, dst, send, recv, to):
        return pltpu.make_async_remote_copy(
            src_ref=src, dst_ref=dst, send_sem=send, recv_sem=recv, device_id=to, device_id_type=MESH
        )

    sent = ([], [], [])

    def start(make, *which, on=2):
        make(*which).start()
        sent[on].append((make, which))

    def wait(dst, recv):
        copy(dst, dst, recv, recv, partner).wait_recv()

    def q_copy(k, other):
        if other:
            return copy(qother, qb.at[INV[k], 1], q_s.at[k, 1], q_r.at[INV[k], 1], x_peer[k][1])
        return copy(qb.at[0, 0], qb.at[INV[k], 0], q_s.at[k, 0], q_r.at[INV[k], 0], x_peer[k][0])

    def q_wait(k, other):
        copy(qb.at[k, other], qb.at[k, other], q_s.at[k, other], q_r.at[k, other], partner).wait_recv()

    def plane(k, g):
        return kv.at[PLANE_AT[k], pl.ds(k % 2 * 4 + 2 * g, 2)]

    def y_copy(k):
        return copy(kv.at[1, 0], kv.at[1, INV[k]], y_s.at[k], y_r.at[INV[k]], y_peer[k])

    def a_copy(k, g):
        if k == 7:
            return copy(plane(5 + g, g), plane(7, g), a_s.at[7, g], a_r.at[7, g], z_down if g else z_up)
        to = z_up if k % 2 == 1 else z_down
        return copy(plane(max(k - 2, 0), g), plane(k, g), a_s.at[k, g], a_r.at[k, g], to)

    def a_hand(k, g):
        return copy(plane(k, g), plane(k, g), ah_s.at[k, g], a_r.at[k, g], partner)

    def pass_a(k, g):
        wait(plane(k, g), a_r.at[k, g])
        if k <= 4:
            start(a_copy, k + 2, g, on=0)
        elif k == 5 + g:
            start(a_copy, 7, g, on=0)
        start(a_hand, k, g, on=0)

    def have_a(*planes):
        @pl.when(c == 1)
        def _():
            for k in planes:
                for g in range(2):
                    wait(plane(k, g), a_r.at[k, g])

    def line(k, g):
        return kv.at[LINE_AT[k], pl.ds(4 * g, 4)]

    def z_copy(k):
        return copy(kv.at[0, 0], kv.at[0, Z_INV[k]], z_s.at[k], z_r.at[Z_INV[k]], z_peer[k])

    def b_copy(k, g):
        if k == 3:
            return copy(line(1 + g, g), line(3, g), b_s.at[3, g], b_r.at[3, g], y_peer[1] if g else y_peer[2])
        return copy(line(0, g), line(INV[k], g), b_s.at[k, g], b_r.at[INV[k], g], y_peer[k])

    def b_hand(k, g):
        return copy(line(k, g), line(k, g), bh_s.at[k, g], b_r.at[k, g], partner)

    def pass_b(k, g):
        wait(line(k, g), b_r.at[k, g])
        if k == 1 + g:
            start(b_copy, 3, g, on=1)
        start(b_hand, k, g, on=1)

    def have_b(*lines):
        @pl.when(c == 0)
        def _():
            for k in lines:
                for g in range(2):
                    wait(line(k, g), b_r.at[k, g])

    def o_copy(k, other):
        return copy(ob.at[k, other], rb.at[INV[k], other], o_s.at[k, other], o_r.at[INV[k], other], x_peer[k][other])

    def o_wait(k, other):
        copy(rb.at[k, other], rb.at[k, other], o_s.at[k, other], o_r.at[k, other], partner).wait_recv()

    def unit(u):
        if isinstance(u, int):
            a, b = divmod(u + 2, 3)
            if u < 4:
                return u, 0
            if u < 16:
                return b + 1, a - 1
            if u < 25:
                return 9 - a, 5 + b
            return 0, u - 24
        a, b = lax.div(u + 2, 3), lax.rem(u + 2, 3)
        from4, from16, from25 = lax.div(u + 28, 32), lax.div(u + 16, 32), lax.div(u + 7, 32)
        query = (1 - from4) * u + (from4 - from16) * (b + 1) + (from16 - from25) * (9 - a)
        slot = (from4 - from16) * (a - 1) + (from16 - from25) * (5 + b) + from25 * (u - 24)
        return query, slot

    lane = lax.broadcasted_iota(jnp.int32, (1, HD), 1)
    ones = jnp.ones((KEYS, HD), jnp.bfloat16)

    key = lax.broadcasted_iota(jnp.int32, (KEYS, HD), 0)
    mark = lax.broadcasted_iota(jnp.int32, (KEYS, HD), 1)
    marked = (lax.div(key, TOK) == mark) & (mark < 8) | (key + 8 == mark) & (key < TOK)
    marks[...] = jnp.where(marked, 1.0, 0.0).astype(jnp.bfloat16)
    token = lax.rem(lax.broadcasted_iota(jnp.int32, (HALF, HD), 0), TOK)
    later = lax.broadcasted_iota(jnp.int32, (HALF, HD), 1) - 8 > token
    triangle[...] = jnp.where(later, MASKED, 0.0).astype(jnp.bfloat16)

    def number_of(ref):
        return ref[...].astype(jnp.float32)[0:1, :]

    def scores(u, s):
        query, slot = unit(u)
        numbers = [number_of(kv.at[slot, i, pl.ds(2 * TOK, 16)]) for i in range(8)]
        rows = []
        for half in range(2):
            mine = number_of(qb.at[query, half, pl.ds(HALF, 16)])
            hidden = jnp.zeros((1, HD), jnp.float32)
            for i in range(8):
                hidden = jnp.where((lane == i) & (numbers[i] > mine), MASKED, hidden)
            same = jnp.where(numbers[0] == mine, 1.0, 0.0).astype(jnp.bfloat16)
            hidden = triangle[...] * same + hidden.astype(jnp.bfloat16)
            rows.append(jnp.concatenate([qb[query, half, 0:HALF, :], hidden], axis=1))
        rows = jnp.concatenate(rows, axis=0)
        keys = jnp.concatenate([kv[slot, :, 0:TOK, :].reshape(KEYS, HD), marks[...]], axis=1)
        s[...] = lax.dot_general(rows, keys, (((1,), (1,)), ((), ())), preferred_element_type=jnp.float32)

    def soften(u, s, p, f):
        query, slot = unit(u)
        for half in range(2):
            at = pl.ds(half * HALF, HALF)
            v = s[at, :]
            old = peak[query, at, :]
            new = jnp.maximum(old, jnp.max(v, axis=1, keepdims=True))
            p[at, :] = jnp.exp2((v - new[:, :1]) * C2).astype(jnp.bfloat16)
            f[at, :] = jnp.exp2((old - new) * C2)
            peak[query, at, :] = new

    def gather(u, p, f):
        query, slot = unit(u)
        vals = kv[slot, :, TOK:2 * TOK, :].reshape(KEYS, HD)
        vals = jnp.concatenate([vals, ones], axis=1)
        factor = jnp.concatenate([f[...], f[...]], axis=1)
        acc[query] = acc[query] * factor + jnp.dot(p[...], vals, preferred_element_type=jnp.float32)

    def finish(k):
        for half in range(2):
            at = pl.ds(half * HALF, HALF)
            total = acc[k, at, HD:2 * HD]
            some = total > 0.0
            safe = jnp.where(some, total, 1.0)
            ob[k, half, 0:HALF, :] = (acc[k, at, 0:HD] / safe).astype(jnp.bfloat16)
            log = jnp.where(some, peak[k, at, :] * SCALE + jnp.log(safe), MASKED)
            hi = log.astype(jnp.bfloat16).astype(jnp.float32)
            mid = (log - hi).astype(jnp.bfloat16).astype(jnp.float32)
            low = log - hi - mid
            packed = jnp.zeros((TOK, HD), jnp.float32)
            for h in range(4):
                for i, term in enumerate((hi, mid, low)):
                    packed = jnp.where(lane == 3 * h + i, term[h * TOK:(h + 1) * TOK, :], packed)
            ob[k, half, HALF:OMSG, :] = packed.astype(jnp.bfloat16)

    def send_out(k):
        finish(k)
        for other in range(2):
            if k or other:
                start(o_copy, k, other)

    pl.semaphore_wait(barrier, 12 + 4 * c)
    start(q_copy, 0, 1)

    @pl.when(c == 0)
    def _():
        for k in (1, 2, 3):
            start(y_copy, k, on=0)

    @pl.when(c == 1)
    def _():
        for k in range(1, 8):
            start(z_copy, k, on=1)

    for k in (1, 2, 3):
        for other in range(2):
            start(q_copy, k, other)

    @pl.when(c == 0)
    def _():
        wait(kv.at[1, 1], y_r.at[1])
        start(a_copy, 1, 0, on=0)
        start(a_copy, 2, 0, on=0)
        start(a_hand, 0, 0, on=0)
        wait(kv.at[1, 2], y_r.at[2])
        wait(kv.at[1, 3], y_r.at[3])
        start(a_copy, 1, 1, on=0)
        start(a_copy, 2, 1, on=0)
        start(a_hand, 0, 1, on=0)

    @pl.when(c == 1)
    def _():
        for g in range(2):
            for k in range(max(4 * g, 1), 4 * g + 4):
                wait(kv.at[0, k], z_r.at[k])
            start(b_copy, 1, g, on=1)
            start(b_copy, 2, g, on=1)
            start(b_hand, 0, g, on=1)

    @pl.when(c == 0)
    def _():
        for g in range(2):
            for k in (1, 2):
                pass_a(k, g)

    have_b(0)
    q_wait(0, 1)
    scores(0, s_a)
    q_wait(1, 0)
    q_wait(1, 1)
    scores(1, s_b)
    soften(0, s_a, p_a, f_a)

    def events(t):
        def at(step, core=None):
            return pl.when(t == step) if core is None else pl.when((t == step) & (c == core))

        @at(0)
        def _():
            for k in (2, 3):
                q_wait(k, 0)
                q_wait(k, 1)

        @at(1)
        def _():
            have_a(0, 1)

        @at(2)
        def _():
            @pl.when(c == 0)
            def _():
                for g in range(2):
                    for k in (3, 4):
                        pass_a(k, g)

            have_a(2, 3)

        @at(3, 1)
        def _():
            for g in range(2):
                for k in (1, 2):
                    pass_b(k, g)

        @at(4)
        def _():
            @pl.when(c == 0)
            def _():
                for g in range(2):
                    for k in (5, 6):
                        pass_a(k, g)

            have_b(1)

        @at(5)
        def _():
            have_b(2)

        @at(6, 1)
        def _():
            for g in range(2):
                pass_b(3, g)

        @at(7)
        def _():
            @pl.when(c == 0)
            def _():
                for g in range(2):
                    pass_a(7, g)

            have_a(4, 5)
            have_b(3)

        @at(8)
        def _():
            have_a(6, 7)

        @at(11)
        def _():
            send_out(3)

        @at(12)
        def _():
            send_out(2)

        @at(14)
        def _():
            send_out(1)

    def turn(t, carry):
        events(t)
        i = 2 * t + 1
        scores(i + 1, s_a)
        soften(i, s_b, p_b, f_b)
        gather(i - 1, p_a, f_a)
        scores(i + 2, s_b)
        soften(i + 1, s_a, p_a, f_a)
        gather(i, p_b, f_b)
        return carry

    lax.fori_loop(0, 15, turn, 0)
    soften(31, s_b, p_b, f_b)
    gather(30, p_a, f_a)
    gather(31, p_b, f_b)
    send_out(0)

    for make, which in sent[2]:
        make(*which).wait_send()
    for core in range(2):
        @pl.when(c == core)
        def _():
            for make, which in sent[core]:
                make(*which).wait_send()
    for k in range(4):
        for other in range(2):
            if k or other:
                o_wait(k, other)

    totals = jnp.zeros((TOK, HD), jnp.float32)
    for other in range(2):
        half = c if other == 0 else 1 - c
        parts = [ob.at[0, 0] if k == 0 and other == 0 else rb.at[k, other] for k in range(4)]
        logs = [part_ref[HALF:OMSG, :].astype(jnp.float32) for part_ref in parts]
        for h in range(4):
            log = [v[:, 3 * h:3 * h + 1] + v[:, 3 * h + 1:3 * h + 2] + v[:, 3 * h + 2:3 * h + 3] for v in logs]
            most = jnp.maximum(jnp.maximum(log[0], log[1]), jnp.maximum(log[2], log[3]))
            share = [jnp.exp(v - most) for v in log]
            whole = share[0] + share[1] + share[2] + share[3]
            mixed = jnp.zeros((TOK, HD), jnp.float32)
            for k in range(4):
                mixed += (share[k] / whole) * parts[k][h * TOK:(h + 1) * TOK, :].astype(jnp.float32)
            att_ref[:, pl.ds(pl.multiple_of((half * 4 + h) * HD, HD), HD)] = mixed
            totals = jnp.where(lane == half * 4 + h, most + jnp.log(whole), totals)
    lt_ref[...] = totals[:, 0:8]


def local(queries, keys, values, block_start):
    vmem = pl.BlockSpec(memory_space=pltpu.VMEM)
    hbm = pl.BlockSpec(memory_space=pl.ANY)
    dma = pltpu.SemaphoreType.DMA
    bf16, f32 = jnp.bfloat16, jnp.float32
    return pl.pallas_call(
        kernel,
        out_shape=(
            jax.ShapeDtypeStruct((TOK, 8 * HD), f32),
            jax.ShapeDtypeStruct((TOK, 8), f32),
        ),
        in_specs=[pl.BlockSpec(memory_space=pltpu.SMEM), hbm, hbm, hbm],
        out_specs=(vmem, vmem),
        scratch_shapes=[
            pltpu.VMEM((TOK, 8 * HD), bf16),
            pltpu.VMEM((8, 8, MSG, HD), bf16),
            pltpu.VMEM((4, 2, QMSG, HD), bf16),
            pltpu.VMEM((QMSG, HD), bf16),
            pltpu.VMEM((4, 2, OMSG, HD), bf16),
            pltpu.VMEM((4, 2, OMSG, HD), bf16),
            pltpu.VMEM((4, ROWS, 2 * HD), f32),
            pltpu.VMEM((4, ROWS, HD), f32),
            pltpu.VMEM((KEYS, HD), bf16),
            pltpu.VMEM((HALF, HD), bf16),
            pltpu.VMEM((ROWS, KEYS), f32),
            pltpu.VMEM((ROWS, KEYS), f32),
            pltpu.VMEM((ROWS, KEYS), bf16),
            pltpu.VMEM((ROWS, KEYS), bf16),
            pltpu.VMEM((ROWS, HD), f32),
            pltpu.VMEM((ROWS, HD), f32),
            dma((4,)), dma((4,)), dma((8,)), dma((8,)), dma((8, 2)), dma((8, 2)),
            dma((4, 2)), dma((4, 2)), dma((8, 2)), dma((4, 2)),
            dma((4, 2)), dma((4, 2)), dma((4, 2)), dma((4, 2)), dma((3,)),
        ],
        compiler_params=pltpu.CompilerParams(
            collective_id=0, has_side_effects=True, vmem_limit_bytes=48 << 20
        ),
    )(block_start, queries, keys, values)


def solution(mesh):
    placed = (
        P(("row", "col"), None),
        P(("row", "col"), None),
        P(("row", "col"), None),
        P(("row", "col")),
    )
    return jax.shard_map(
        local,
        mesh=mesh,
        in_specs=placed,
        out_specs=(P(("row", "col"), None), P(("row", "col"), None)),
        check_vma=False,
    )
```

```python
import functools
import math

import jax
import jax.numpy as jnp
from jax import lax
from jax.experimental import pallas as pl
from jax.experimental.pallas import tpu as pltpu
from jax.sharding import PartitionSpec as P

MESH = pl.DeviceIdType.MESH
TOK = 96
HD = 128
HALF = 4 * TOK
MSG = 2 * TOK + 16
QMSG = HALF + 16
OMSG = HALF + 16
ROWS = 2 * HALF
KEYS = 8 * TOK
REL = (0, 1, 3, 2)
INV = (0, 2, 1, 3)
Z_OFF = (0, 1, 7, 2, 6, 3, 5, 4)
Z_INV = (0, 2, 1, 4, 3, 6, 5, 7)
PLANE_AT = ((0, 0), (1, 4), (2, 0), (2, 4), (5, 0), (5, 4), (7, 0), (7, 4))
Z_AT = ((1, 0), (0, 4), (0, 5), (0, 6), (0, 7), (1, 1), (1, 2), (1, 3))
LINE_AT = (None, 3, 4, 6)
SCALE = HD ** -0.5
C2 = SCALE * math.log2(math.e)
MASKED = -1e30
FLOOR = -1e20


def kernel(start_ref, q_hbm, k_hbm, v_hbm, att_ref, lt_ref, q_ref, kv, qb, qother, ob, rb, acc, peak,
           marks, triangle, s_a, s_b, p_a, p_b, f_a, f_b,
           y_s, y_r, z_s, z_r, a_s, a_r, b_s, b_r, ah_s, bh_s, q_s, q_r, o_s, o_r, in_s):
    row = lax.axis_index("row")
    col = lax.axis_index("col")
    x = lax.rem(row, 4)
    y = lax.div(col, 16) * 2 + lax.div(row, 4)
    z = lax.rem(lax.div(col, 2), 8)
    c = lax.rem(col, 2)

    def device(xx, yy, zz, cc):
        return (lax.rem(yy, 2) * 4 + xx, (lax.div(yy, 2) * 8 + zz) * 2 + cc)

    partner = device(x, y, z, 1 - c)
    y_peer = [None] + [device(x, lax.rem(y + REL[k], 4), z, c) for k in (1, 2, 3)]
    z_up = device(x, y, lax.rem(z + 1, 8), c)
    z_down = device(x, y, lax.rem(z + 7, 8), c)
    z_peer = [device(x, y, lax.rem(z + step, 8), c) for step in Z_OFF]
    x_peer = [[None, partner]] + [
        [device(lax.rem(x + REL[k], 4), y, z, c), device(lax.rem(x + REL[k], 4), y, z, 1 - c)]
        for k in (1, 2, 3)
    ]

    barrier = pltpu.get_barrier_semaphore()

    def greet(peers):
        for peer in peers:
            pl.semaphore_signal(barrier, inc=1, device_id=peer, device_id_type=MESH)

    greet([partner, z_up, z_down, y_peer[1], y_peer[2]] + x_peer[1] + x_peer[2] + x_peer[3])

    @pl.when(c == 0)
    def _():
        greet([y_peer[3]])

    @pl.when(c == 1)
    def _():
        greet(z_peer[3:])

    loads = [
        pltpu.make_async_copy(k_hbm, kv.at[c, 0, pl.ds(0, TOK)], in_s.at[0]),
        pltpu.make_async_copy(v_hbm, kv.at[c, 0, pl.ds(TOK, TOK)], in_s.at[1]),
        pltpu.make_async_copy(q_hbm, q_ref, in_s.at[2]),
    ]
    for load in loads:
        load.start()
    acc[...] = jnp.zeros_like(acc)
    peak[...] = jnp.full(peak.shape, FLOOR, jnp.float32)

    number = jnp.full((16, HD), start_ref[0].astype(jnp.float32), jnp.float32).astype(jnp.bfloat16)
    kv[c, 0, 2 * TOK:MSG, :] = number
    for load in loads:
        load.wait()
    for h in range(4):
        here = pl.ds(pl.multiple_of((c * 4 + h) * HD, HD), HD)
        there = pl.ds(pl.multiple_of(((1 - c) * 4 + h) * HD, HD), HD)
        qb[0, 0, h * TOK:(h + 1) * TOK, :] = q_ref[:, here]
        qother[h * TOK:(h + 1) * TOK, :] = q_ref[:, there]
    qb[0, 0, HALF:QMSG, :] = number
    qother[HALF:QMSG, :] = number

    def copy(src, dst, send, recv, to):
        return pltpu.make_async_remote_copy(
            src_ref=src, dst_ref=dst, send_sem=send, recv_sem=recv, device_id=to, device_id_type=MESH
        )

    sent = ([], [], [])

    def start(make, *which, on=2):
        make(*which).start()
        sent[on].append((make, which))

    def wait(dst, recv):
        copy(dst, dst, recv, recv, partner).wait_recv()

    def q_copy(k, other):
        if other:
            return copy(qother, qb.at[INV[k], 1], q_s.at[k, 1], q_r.at[INV[k], 1], x_peer[k][1])
        return copy(qb.at[0, 0], qb.at[INV[k], 0], q_s.at[k, 0], q_r.at[INV[k], 0], x_peer[k][0])

    def q_wait(k, other):
        copy(qb.at[k, other], qb.at[k, other], q_s.at[k, other], q_r.at[k, other], partner).wait_recv()

    def plane(k, g):
        unit, first = PLANE_AT[k]
        return kv.at[unit, pl.ds(first + 2 * g, 2)]

    def y_copy(k):
        return copy(kv.at[0, 0], kv.at[0, INV[k]], y_s.at[k], y_r.at[INV[k]], y_peer[k])

    def a_copy(k, g):
        if k == 7:
            return copy(plane(5 + g, g), plane(7, g), a_s.at[7, g], a_r.at[7, g], z_down if g else z_up)
        to = z_up if k % 2 == 1 else z_down
        return copy(plane(max(k - 2, 0), g), plane(k, g), a_s.at[k, g], a_r.at[k, g], to)

    def a_hand(k, g):
        return copy(plane(k, g), plane(k, g), ah_s.at[k, g], a_r.at[k, g], partner)

    def pass_a(k, g):
        wait(plane(k, g), a_r.at[k, g])
        if k <= 4:
            start(a_copy, k + 2, g, on=0)
        elif k == 5 + g:
            start(a_copy, 7, g, on=0)
        start(a_hand, k, g, on=0)

    def have_a(*planes):
        @pl.when(c == 1)
        def _():
            for k in planes:
                for g in range(2):
                    wait(plane(k, g), a_r.at[k, g])

    def line(k, g):
        if k == 0:
            return kv.at[g, pl.ds(4 - 4 * g, 4)]
        return kv.at[LINE_AT[k], pl.ds(4 * g, 4)]

    def z_copy(k):
        return copy(kv.at[1, 0], kv.at[Z_AT[Z_INV[k]]], z_s.at[k], z_r.at[Z_INV[k]], z_peer[k])

    def b_copy(k, g):
        if k == 3:
            return copy(line(1 + g, g), line(3, g), b_s.at[3, g], b_r.at[3, g], y_peer[1] if g else y_peer[2])
        return copy(line(0, g), line(INV[k], g), b_s.at[k, g], b_r.at[INV[k], g], y_peer[k])

    def b_hand(k, g):
        return copy(line(k, g), line(k, g), bh_s.at[k, g], b_r.at[k, g], partner)

    def pass_b(k, g):
        wait(line(k, g), b_r.at[k, g])
        if k == 1 + g:
            start(b_copy, 3, g, on=1)
        start(b_hand, k, g, on=1)

    def have_b(k, parts=(0, 1)):
        @pl.when(c == 0)
        def _():
            for g in parts:
                wait(line(k, g), b_r.at[k, g])

    def o_copy(k, other):
        return copy(ob.at[k, other], rb.at[INV[k], other], o_s.at[k, other], o_r.at[INV[k], other], x_peer[k][other])

    def o_wait(k, other):
        copy(rb.at[k, other], rb.at[k, other], o_s.at[k, other], o_r.at[k, other], partner).wait_recv()

    def unit(u):
        if isinstance(u, int):
            if u < 8:
                return u % 4, u // 4
            if u < 14:
                return (u + 1) % 3 + 1, (u + 1) // 3 - 1
            if u < 26:
                return 7 - (u + 2) // 4, 4 + (u + 2) % 4
            return 0, u - 24
        from8, from14, from26 = (lax.div(u + 32 - n, 32) for n in (8, 14, 26))
        query = (
            (1 - from8) * lax.rem(u, 4)
            + (from8 - from14) * (lax.rem(u + 1, 3) + 1) + (from14 - from26) * (7 - lax.div(u + 2, 4))
        )
        slot = (
            (1 - from8) * lax.div(u, 4)
            + (from8 - from14) * (lax.div(u + 1, 3) - 1) + (from14 - from26) * (4 + lax.rem(u + 2, 4)) + from26 * (u - 24)
        )
        return query, slot

    lane = lax.broadcasted_iota(jnp.int32, (1, HD), 1)
    ones = jnp.ones((KEYS, HD), jnp.bfloat16)

    key = lax.broadcasted_iota(jnp.int32, (KEYS, HD), 0)
    mark = lax.broadcasted_iota(jnp.int32, (KEYS, HD), 1)
    marked = (lax.div(key, TOK) == mark) & (mark < 8) | (key + 8 == mark) & (key < TOK)
    marks[...] = jnp.where(marked, 1.0, 0.0).astype(jnp.bfloat16)
    token = lax.rem(lax.broadcasted_iota(jnp.int32, (HALF, HD), 0), TOK)
    later = lax.broadcasted_iota(jnp.int32, (HALF, HD), 1) - 8 > token
    triangle[...] = jnp.where(later, MASKED, 0.0).astype(jnp.bfloat16)

    def number_of(ref):
        return ref[...].astype(jnp.float32)[0:1, :]

    def scores(u, s):
        query, slot = unit(u)
        numbers = [number_of(kv.at[slot, i, pl.ds(2 * TOK, 16)]) for i in range(8)]
        rows = []
        for half in range(2):
            mine = number_of(qb.at[query, half, pl.ds(HALF, 16)])
            hidden = jnp.zeros((1, HD), jnp.float32)
            for i in range(8):
                hidden = jnp.where((lane == i) & (numbers[i] > mine), MASKED, hidden)
            same = jnp.where(numbers[0] == mine, 1.0, 0.0).astype(jnp.bfloat16)
            hidden = triangle[...] * same + hidden.astype(jnp.bfloat16)
            rows.append(jnp.concatenate([qb[query, half, 0:HALF, :], hidden], axis=1))
        rows = jnp.concatenate(rows, axis=0)
        keys = jnp.concatenate([kv[slot, :, 0:TOK, :].reshape(KEYS, HD), marks[...]], axis=1)
        s[...] = lax.dot_general(rows, keys, (((1,), (1,)), ((), ())), preferred_element_type=jnp.float32)

    def soften(u, s, p, f):
        query, slot = unit(u)
        for half in range(2):
            at = pl.ds(half * HALF, HALF)
            v = s[at, :]
            old = peak[query, at, :]
            new = jnp.maximum(old, jnp.max(v, axis=1, keepdims=True))
            p[at, :] = jnp.exp2((v - new[:, :1]) * C2).astype(jnp.bfloat16)
            f[at, :] = jnp.exp2((old - new) * C2)
            peak[query, at, :] = new

    def gather(u, p, f):
        query, slot = unit(u)
        vals = kv[slot, :, TOK:2 * TOK, :].reshape(KEYS, HD)
        vals = jnp.concatenate([vals, ones], axis=1)
        factor = jnp.concatenate([f[...], f[...]], axis=1)
        acc[query] = acc[query] * factor + jnp.dot(p[...], vals, preferred_element_type=jnp.float32)

    def finish(k):
        for half in range(2):
            at = pl.ds(half * HALF, HALF)
            total = acc[k, at, HD:2 * HD]
            some = total > 0.0
            safe = jnp.where(some, total, 1.0)
            ob[k, half, 0:HALF, :] = (acc[k, at, 0:HD] / safe).astype(jnp.bfloat16)
            log = jnp.where(some, peak[k, at, :] * SCALE + jnp.log(safe), MASKED)
            hi = log.astype(jnp.bfloat16).astype(jnp.float32)
            mid = (log - hi).astype(jnp.bfloat16).astype(jnp.float32)
            low = log - hi - mid
            packed = jnp.zeros((TOK, HD), jnp.float32)
            for h in range(4):
                for i, term in enumerate((hi, mid, low)):
                    packed = jnp.where(lane == 3 * h + i, term[h * TOK:(h + 1) * TOK, :], packed)
            packed = jnp.concatenate([packed, jnp.zeros((HD - TOK, HD), jnp.float32)], axis=0)
            ob[k, half, HALF:OMSG, :] = packed.T[0:16, :].astype(jnp.bfloat16)

    def send_out(k):
        finish(k)
        for other in range(2):
            if k or other:
                start(o_copy, k, other)

    pl.semaphore_wait(barrier, 12 + 4 * c)
    start(q_copy, 0, 1)

    @pl.when(c == 0)
    def _():
        for k in (1, 2, 3):
            start(y_copy, k, on=0)

    @pl.when(c == 1)
    def _():
        for k in range(1, 8):
            start(z_copy, k, on=1)

    for k in (1, 2):
        for other in range(2):
            start(q_copy, k, other)

    @pl.when(c == 0)
    def _():
        wait(kv.at[0, 1], y_r.at[1])
        start(a_copy, 1, 0, on=0)
        start(a_copy, 2, 0, on=0)
        start(a_hand, 0, 0, on=0)
        wait(kv.at[0, 2], y_r.at[2])
        wait(kv.at[0, 3], y_r.at[3])
        start(a_copy, 1, 1, on=0)
        start(a_copy, 2, 1, on=0)
        start(a_hand, 0, 1, on=0)

    def line_done(g):
        for k in (range(5, 8) if g else range(1, 5)):
            wait(kv.at[Z_AT[k]], z_r.at[k])
        start(b_copy, 1, g, on=1)
        start(b_copy, 2, g, on=1)
        start(b_hand, 0, g, on=1)

    @pl.when(c == 1)
    def _():
        line_done(0)

    for other in range(2):
        start(q_copy, 3, other)
    have_a(0)
    have_b(0, (0,))
    q_wait(0, 1)
    scores(0, s_a)
    soften(0, s_a, p_a, f_a)
    q_wait(1, 0)
    q_wait(1, 1)
    scores(1, s_b)
    q_wait(2, 0)
    q_wait(2, 1)
    scores(2, s_a)
    soften(1, s_b, p_b, f_b)
    gather(0, p_a, f_a)

    @pl.when(c == 0)
    def _():
        for g in range(2):
            for k in (1, 2):
                pass_a(k, g)

    @pl.when(c == 1)
    def _():
        line_done(1)

    q_wait(3, 0)
    q_wait(3, 1)
    scores(3, s_b)
    soften(2, s_a, p_a, f_a)
    gather(1, p_b, f_b)

    def events(t):
        def at(step, core=None):
            return pl.when(t == step) if core is None else pl.when((t == step) & (c == core))

        @at(1)
        def _():
            have_a(1)
            have_b(0, (1,))

        @at(1, 0)
        def _():
            for g in range(2):
                for k in (3, 4):
                    pass_a(k, g)

        @at(2, 1)
        def _():
            for g in range(2):
                for k in (1, 2):
                    pass_b(k, g)

        @at(3, 0)
        def _():
            for g in range(2):
                for k in (5, 6):
                    pass_a(k, g)

        @at(3)
        def _():
            have_a(2, 3)

        @at(4)
        def _():
            have_b(1)

        @at(4, 1)
        def _():
            for g in range(2):
                pass_b(3, g)

        @at(5, 0)
        def _():
            for g in range(2):
                pass_a(7, g)

        @at(6)
        def _():
            have_b(2)
            have_a(4, 5)

        @at(7)
        def _():
            have_b(3)
            have_a(6, 7)

        @at(9)
        def _():
            send_out(3)

        @at(11)
        def _():
            send_out(2)

        @at(13)
        def _():
            send_out(1)

    def turn(t, carry):
        events(t)
        i = 2 * t + 1
        scores(i + 1, s_a)
        soften(i, s_b, p_b, f_b)
        gather(i - 1, p_a, f_a)
        scores(i + 2, s_b)
        soften(i + 1, s_a, p_a, f_a)
        gather(i, p_b, f_b)
        return carry

    lax.fori_loop(1, 15, turn, 0)
    soften(31, s_b, p_b, f_b)
    gather(30, p_a, f_a)
    gather(31, p_b, f_b)
    send_out(0)

    for make, which in sent[2]:
        make(*which).wait_send()
    for core in range(2):
        @pl.when(c == core)
        def _():
            for make, which in sent[core]:
                make(*which).wait_send()
    for k in range(4):
        for other in range(2):
            if k or other:
                o_wait(k, other)

    sub = lax.broadcasted_iota(jnp.int32, (16, HD), 0)
    totals = jnp.zeros((16, HD), jnp.float32)
    for other in range(2):
        half = c if other == 0 else 1 - c
        parts = [ob.at[0, 0] if k == 0 and other == 0 else rb.at[k, other] for k in range(4)]
        logs = [part_ref[HALF:OMSG, :].astype(jnp.float32) for part_ref in parts]
        shares = jnp.zeros((16, HD), jnp.float32)
        for h in range(4):
            log = [v[3 * h:3 * h + 1, :] + v[3 * h + 1:3 * h + 2, :] + v[3 * h + 2:3 * h + 3, :] for v in logs]
            most = jnp.maximum(jnp.maximum(log[0], log[1]), jnp.maximum(log[2], log[3]))
            share = [jnp.exp(v - most) for v in log]
            whole = share[0] + share[1] + share[2] + share[3]
            for k in range(4):
                shares = jnp.where(sub == 4 * h + k, share[k] / whole, shares)
            totals = jnp.where(sub == half * 4 + h, most + jnp.log(whole), totals)
        shares = jnp.concatenate([shares, jnp.zeros((HD - 16, HD), jnp.float32)], axis=0).T
        for h in range(4):
            mixed = jnp.zeros((TOK, HD), jnp.float32)
            for k in range(4):
                share = shares[0:TOK, 4 * h + k:4 * h + k + 1]
                mixed += share * parts[k][h * TOK:(h + 1) * TOK, :].astype(jnp.float32)
            att_ref[:, pl.ds(pl.multiple_of((half * 4 + h) * HD, HD), HD)] = mixed
    lt_ref[...] = totals[0:8, 0:TOK]


def local(queries, keys, values, block_start):
    vmem = pl.BlockSpec(memory_space=pltpu.VMEM)
    hbm = pl.BlockSpec(memory_space=pl.ANY)
    dma = pltpu.SemaphoreType.DMA
    bf16, f32 = jnp.bfloat16, jnp.float32
    attended, log_total = pl.pallas_call(
        kernel,
        out_shape=(
            jax.ShapeDtypeStruct((TOK, 8 * HD), f32),
            jax.ShapeDtypeStruct((8, TOK), f32),
        ),
        in_specs=[pl.BlockSpec(memory_space=pltpu.SMEM), hbm, hbm, hbm],
        out_specs=(vmem, vmem),
        scratch_shapes=[
            pltpu.VMEM((TOK, 8 * HD), bf16),
            pltpu.VMEM((8, 8, MSG, HD), bf16),
            pltpu.VMEM((4, 2, QMSG, HD), bf16),
            pltpu.VMEM((QMSG, HD), bf16),
            pltpu.VMEM((4, 2, OMSG, HD), bf16),
            pltpu.VMEM((4, 2, OMSG, HD), bf16),
            pltpu.VMEM((4, ROWS, 2 * HD), f32),
            pltpu.VMEM((4, ROWS, HD), f32),
            pltpu.VMEM((KEYS, HD), bf16),
            pltpu.VMEM((HALF, HD), bf16),
            pltpu.VMEM((ROWS, KEYS), f32),
            pltpu.VMEM((ROWS, KEYS), f32),
            pltpu.VMEM((ROWS, KEYS), bf16),
            pltpu.VMEM((ROWS, KEYS), bf16),
            pltpu.VMEM((ROWS, HD), f32),
            pltpu.VMEM((ROWS, HD), f32),
            dma((4,)), dma((4,)), dma((8,)), dma((8,)), dma((8, 2)), dma((8, 2)),
            dma((4, 2)), dma((4, 2)), dma((8, 2)), dma((4, 2)),
            dma((4, 2)), dma((4, 2)), dma((4, 2)), dma((4, 2)), dma((3,)),
        ],
        compiler_params=pltpu.CompilerParams(
            collective_id=0, has_side_effects=True, vmem_limit_bytes=48 << 20
        ),
    )(block_start, queries, keys, values)
    return attended, log_total.T


def solution(mesh):
    placed = (
        P(("row", "col"), None),
        P(("row", "col"), None),
        P(("row", "col"), None),
        P(("row", "col")),
    )
    return jax.shard_map(
        local,
        mesh=mesh,
        in_specs=placed,
        out_specs=(P(("row", "col"), None), P(("row", "col"), None)),
        check_vma=False,
    )
```

```python
import functools
import math

import jax
import jax.numpy as jnp
from jax import lax
from jax.experimental import pallas as pl
from jax.experimental.pallas import tpu as pltpu
from jax.sharding import PartitionSpec as P

MESH = pl.DeviceIdType.MESH
TOK = 96
HD = 128
HALF = 4 * TOK
MSG = 2 * TOK + 16
QMSG = HALF + 16
OMSG = HALF + 16
ROWS = 2 * HALF
KEYS = 8 * TOK
REL = (0, 1, 3, 2)
INV = (0, 2, 1, 3)
Z_OFF = (0, 1, 7, 2, 6, 3, 5, 4)
Z_INV = (0, 2, 1, 4, 3, 6, 5, 7)
PLANE_AT = ((0, 0), (1, 4), (2, 0), (2, 4), (5, 0), (5, 4), (7, 0), (7, 4))
Z_AT = ((1, 0), (0, 4), (0, 5), (0, 6), (0, 7), (1, 1), (1, 2), (1, 3))
LINE_AT = (None, 3, 4, 6)
SCALE = HD ** -0.5
C2 = SCALE * math.log2(math.e)
MASKED = -1e30
FLOOR = -1e20


def kernel(start_ref, q_hbm, k_hbm, v_hbm, att_ref, lt_ref, q_ref, kv, qb, qother, ob, rb, acc, peak,
           marks, triangle, s_a, s_b, p_a, p_b, f_a, f_b,
           y_s, y_r, z_s, z_r, a_s, a_r, b_s, b_r, ah_s, bh_s, q_s, q_r, o_s, o_r, in_s):
    row = lax.axis_index("row")
    col = lax.axis_index("col")
    x = lax.rem(row, 4)
    y = lax.div(col, 16) * 2 + lax.div(row, 4)
    z = lax.rem(lax.div(col, 2), 8)
    c = lax.rem(col, 2)

    def device(xx, yy, zz, cc):
        return (lax.rem(yy, 2) * 4 + xx, (lax.div(yy, 2) * 8 + zz) * 2 + cc)

    partner = device(x, y, z, 1 - c)
    y_peer = [None] + [device(x, lax.rem(y + REL[k], 4), z, c) for k in (1, 2, 3)]
    z_up = device(x, y, lax.rem(z + 1, 8), c)
    z_down = device(x, y, lax.rem(z + 7, 8), c)
    z_peer = [device(x, y, lax.rem(z + step, 8), c) for step in Z_OFF]
    x_peer = [[None, partner]] + [
        [device(lax.rem(x + REL[k], 4), y, z, c), device(lax.rem(x + REL[k], 4), y, z, 1 - c)]
        for k in (1, 2, 3)
    ]

    barrier = pltpu.get_barrier_semaphore()

    def greet(peers):
        for peer in peers:
            pl.semaphore_signal(barrier, inc=1, device_id=peer, device_id_type=MESH)

    greet([partner, z_up, z_down, y_peer[1], y_peer[2]] + x_peer[1] + x_peer[2] + x_peer[3])

    @pl.when(c == 0)
    def _():
        greet([y_peer[3]])

    @pl.when(c == 1)
    def _():
        greet(z_peer[3:])

    loads = [
        pltpu.make_async_copy(k_hbm, kv.at[c, 0, pl.ds(0, TOK)], in_s.at[0]),
        pltpu.make_async_copy(v_hbm, kv.at[c, 0, pl.ds(TOK, TOK)], in_s.at[1]),
        pltpu.make_async_copy(q_hbm, q_ref, in_s.at[2]),
    ]
    for load in loads:
        load.start()

    number = jnp.full((16, HD), start_ref[0].astype(jnp.float32), jnp.float32).astype(jnp.bfloat16)
    kv[c, 0, 2 * TOK:MSG, :] = number
    for load in loads[:2]:
        load.wait()

    def copy(src, dst, send, recv, to):
        return pltpu.make_async_remote_copy(
            src_ref=src, dst_ref=dst, send_sem=send, recv_sem=recv, device_id=to, device_id_type=MESH
        )

    sent = ([], [], [])

    def start(make, *which, on=2):
        make(*which).start()
        sent[on].append((make, which))

    def wait(dst, recv):
        copy(dst, dst, recv, recv, partner).wait_recv()

    def q_copy(k, other):
        if other:
            return copy(qother, qb.at[INV[k], 1], q_s.at[k, 1], q_r.at[INV[k], 1], x_peer[k][1])
        return copy(qb.at[0, 0], qb.at[INV[k], 0], q_s.at[k, 0], q_r.at[INV[k], 0], x_peer[k][0])

    def q_wait(k, other):
        copy(qb.at[k, other], qb.at[k, other], q_s.at[k, other], q_r.at[k, other], partner).wait_recv()

    def plane(k, g):
        unit, first = PLANE_AT[k]
        return kv.at[unit, pl.ds(first + 2 * g, 2)]

    def y_copy(k):
        return copy(kv.at[0, 0], kv.at[0, INV[k]], y_s.at[k], y_r.at[INV[k]], y_peer[k])

    def a_copy(k, g):
        if k == 7:
            return copy(plane(5 + g, g), plane(7, g), a_s.at[7, g], a_r.at[7, g], z_down if g else z_up)
        to = z_up if k % 2 == 1 else z_down
        return copy(plane(max(k - 2, 0), g), plane(k, g), a_s.at[k, g], a_r.at[k, g], to)

    def a_hand(k, g):
        return copy(plane(k, g), plane(k, g), ah_s.at[k, g], a_r.at[k, g], partner)

    def pass_a(k, g):
        wait(plane(k, g), a_r.at[k, g])
        if k <= 4:
            start(a_copy, k + 2, g, on=0)
        elif k == 5 + g:
            start(a_copy, 7, g, on=0)
        start(a_hand, k, g, on=0)

    def have_a(*planes):
        @pl.when(c == 1)
        def _():
            for k in planes:
                for g in range(2):
                    wait(plane(k, g), a_r.at[k, g])

    def line(k, g):
        if k == 0:
            return kv.at[g, pl.ds(4 - 4 * g, 4)]
        return kv.at[LINE_AT[k], pl.ds(4 * g, 4)]

    def z_copy(k):
        return copy(kv.at[1, 0], kv.at[Z_AT[Z_INV[k]]], z_s.at[k], z_r.at[Z_INV[k]], z_peer[k])

    def b_copy(k, g):
        if k == 3:
            return copy(line(1 + g, g), line(3, g), b_s.at[3, g], b_r.at[3, g], y_peer[1] if g else y_peer[2])
        return copy(line(0, g), line(INV[k], g), b_s.at[k, g], b_r.at[INV[k], g], y_peer[k])

    def b_hand(k, g):
        return copy(line(k, g), line(k, g), bh_s.at[k, g], b_r.at[k, g], partner)

    def pass_b(k, g):
        wait(line(k, g), b_r.at[k, g])
        if k == 1 + g:
            start(b_copy, 3, g, on=1)
        start(b_hand, k, g, on=1)

    def have_b(k, parts=(0, 1)):
        @pl.when(c == 0)
        def _():
            for g in parts:
                wait(line(k, g), b_r.at[k, g])

    def o_copy(k, other):
        return copy(ob.at[k, other], rb.at[INV[k], other], o_s.at[k, other], o_r.at[INV[k], other], x_peer[k][other])

    def o_wait(k, other):
        copy(rb.at[k, other], rb.at[k, other], o_s.at[k, other], o_r.at[k, other], partner).wait_recv()

    def unit(u):
        if isinstance(u, int):
            if u < 8:
                return u % 4, u // 4
            if u < 14:
                return (u + 1) % 3 + 1, (u + 1) // 3 - 1
            if u < 26:
                return 7 - (u + 2) // 4, 4 + (u + 2) % 4
            return 0, u - 24
        from8, from14, from26 = (lax.div(u + 32 - n, 32) for n in (8, 14, 26))
        query = (
            (1 - from8) * lax.rem(u, 4)
            + (from8 - from14) * (lax.rem(u + 1, 3) + 1) + (from14 - from26) * (7 - lax.div(u + 2, 4))
        )
        slot = (
            (1 - from8) * lax.div(u, 4)
            + (from8 - from14) * (lax.div(u + 1, 3) - 1) + (from14 - from26) * (4 + lax.rem(u + 2, 4)) + from26 * (u - 24)
        )
        return query, slot

    lane = lax.broadcasted_iota(jnp.int32, (1, HD), 1)
    ones = jnp.ones((KEYS, HD), jnp.bfloat16)

    def number_of(ref):
        return ref[...].astype(jnp.float32)[0:1, :]

    def scores(u, s):
        query, slot = unit(u)
        numbers = [number_of(kv.at[slot, i, pl.ds(2 * TOK, 16)]) for i in range(8)]
        rows = []
        for half in range(2):
            mine = number_of(qb.at[query, half, pl.ds(HALF, 16)])
            hidden = jnp.zeros((1, HD), jnp.float32)
            for i in range(8):
                hidden = jnp.where((lane == i) & (numbers[i] > mine), MASKED, hidden)
            same = jnp.where(numbers[0] == mine, 1.0, 0.0).astype(jnp.bfloat16)
            hidden = triangle[...] * same + hidden.astype(jnp.bfloat16)
            rows.append(jnp.concatenate([qb[query, half, 0:HALF, :], hidden], axis=1))
        rows = jnp.concatenate(rows, axis=0)
        keys = jnp.concatenate([kv[slot, :, 0:TOK, :].reshape(KEYS, HD), marks[...]], axis=1)
        s[...] = lax.dot_general(rows, keys, (((1,), (1,)), ((), ())), preferred_element_type=jnp.float32)

    def soften(u, s, p, f):
        query, slot = unit(u)
        for half in range(2):
            at = pl.ds(half * HALF, HALF)
            v = s[at, :]
            old = peak[query, at, :]
            new = jnp.maximum(old, jnp.max(v, axis=1, keepdims=True))
            p[at, :] = jnp.exp2((v - new[:, :1]) * C2).astype(jnp.bfloat16)
            f[at, :] = jnp.exp2((old - new) * C2)
            peak[query, at, :] = new

    def gather(u, p, f):
        query, slot = unit(u)
        vals = kv[slot, :, TOK:2 * TOK, :].reshape(KEYS, HD)
        vals = jnp.concatenate([vals, ones], axis=1)
        factor = jnp.concatenate([f[...], f[...]], axis=1)
        acc[query] = acc[query] * factor + jnp.dot(p[...], vals, preferred_element_type=jnp.float32)

    def finish(k):
        for half in range(2):
            at = pl.ds(half * HALF, HALF)
            total = acc[k, at, HD:2 * HD]
            some = total > 0.0
            safe = jnp.where(some, total, 1.0)
            ob[k, half, 0:HALF, :] = (acc[k, at, 0:HD] / safe).astype(jnp.bfloat16)
            log = jnp.where(some, peak[k, at, :] * SCALE + jnp.log(safe), MASKED)
            hi = log.astype(jnp.bfloat16).astype(jnp.float32)
            mid = (log - hi).astype(jnp.bfloat16).astype(jnp.float32)
            low = log - hi - mid
            packed = jnp.zeros((TOK, HD), jnp.float32)
            for h in range(4):
                for i, term in enumerate((hi, mid, low)):
                    packed = jnp.where(lane == 3 * h + i, term[h * TOK:(h + 1) * TOK, :], packed)
            packed = jnp.concatenate([packed, jnp.zeros((HD - TOK, HD), jnp.float32)], axis=0)
            ob[k, half, HALF:OMSG, :] = packed.T[0:16, :].astype(jnp.bfloat16)

    def send_out(k):
        finish(k)
        for other in range(2):
            if k or other:
                start(o_copy, k, other)

    pl.semaphore_wait(barrier, 12 + 4 * c)

    @pl.when(c == 0)
    def _():
        for k in (1, 2, 3):
            start(y_copy, k, on=0)

    @pl.when(c == 1)
    def _():
        for k in range(1, 8):
            start(z_copy, k, on=1)

    loads[2].wait()
    for h in range(4):
        here = pl.ds(pl.multiple_of((c * 4 + h) * HD, HD), HD)
        there = pl.ds(pl.multiple_of(((1 - c) * 4 + h) * HD, HD), HD)
        qb[0, 0, h * TOK:(h + 1) * TOK, :] = q_ref[:, here]
        qother[h * TOK:(h + 1) * TOK, :] = q_ref[:, there]
    qb[0, 0, HALF:QMSG, :] = number
    qother[HALF:QMSG, :] = number
    start(q_copy, 0, 1)
    for k in (1, 2):
        for other in range(2):
            start(q_copy, k, other)

    acc[...] = jnp.zeros_like(acc)
    peak[...] = jnp.full(peak.shape, FLOOR, jnp.float32)
    key = lax.broadcasted_iota(jnp.int32, (KEYS, HD), 0)
    mark = lax.broadcasted_iota(jnp.int32, (KEYS, HD), 1)
    marked = (lax.div(key, TOK) == mark) & (mark < 8) | (key + 8 == mark) & (key < TOK)
    marks[...] = jnp.where(marked, 1.0, 0.0).astype(jnp.bfloat16)
    token = lax.rem(lax.broadcasted_iota(jnp.int32, (HALF, HD), 0), TOK)
    later = lax.broadcasted_iota(jnp.int32, (HALF, HD), 1) - 8 > token
    triangle[...] = jnp.where(later, MASKED, 0.0).astype(jnp.bfloat16)

    @pl.when(c == 0)
    def _():
        wait(kv.at[0, 1], y_r.at[1])
        start(a_copy, 1, 0, on=0)
        start(a_copy, 2, 0, on=0)
        start(a_hand, 0, 0, on=0)
        wait(kv.at[0, 2], y_r.at[2])
        wait(kv.at[0, 3], y_r.at[3])
        start(a_copy, 1, 1, on=0)
        start(a_copy, 2, 1, on=0)
        start(a_hand, 0, 1, on=0)

    def line_done(g):
        for k in (range(5, 8) if g else range(1, 5)):
            wait(kv.at[Z_AT[k]], z_r.at[k])
        start(b_copy, 1, g, on=1)
        start(b_copy, 2, g, on=1)
        start(b_hand, 0, g, on=1)

    @pl.when(c == 1)
    def _():
        line_done(0)

    for other in range(2):
        start(q_copy, 3, other)
    have_a(0)
    have_b(0, (0,))
    q_wait(0, 1)
    scores(0, s_a)
    soften(0, s_a, p_a, f_a)
    q_wait(1, 0)
    q_wait(1, 1)
    scores(1, s_b)
    q_wait(2, 0)
    q_wait(2, 1)
    scores(2, s_a)
    soften(1, s_b, p_b, f_b)
    gather(0, p_a, f_a)

    @pl.when(c == 0)
    def _():
        for g in range(2):
            for k in (1, 2):
                pass_a(k, g)

    @pl.when(c == 1)
    def _():
        line_done(1)

    q_wait(3, 0)
    q_wait(3, 1)
    scores(3, s_b)
    soften(2, s_a, p_a, f_a)
    gather(1, p_b, f_b)

    def events(t):
        def at(step, core=None):
            return pl.when(t == step) if core is None else pl.when((t == step) & (c == core))

        @at(1)
        def _():
            have_a(1)
            have_b(0, (1,))

        @at(2, 0)
        def _():
            for g in range(2):
                for k in (3, 4):
                    pass_a(k, g)

        @at(3, 1)
        def _():
            for g in range(2):
                for k in (1, 2):
                    pass_b(k, g)

        @at(4, 0)
        def _():
            for g in range(2):
                for k in (5, 6):
                    pass_a(k, g)

        @at(3)
        def _():
            have_a(2, 3)

        @at(4)
        def _():
            have_b(1)

        @at(5, 1)
        def _():
            for g in range(2):
                pass_b(3, g)

        @at(6, 0)
        def _():
            for g in range(2):
                pass_a(7, g)

        @at(6)
        def _():
            have_b(2)
            have_a(4, 5)

        @at(7)
        def _():
            have_b(3)
            have_a(6, 7)

        @at(9)
        def _():
            send_out(3)

        @at(11)
        def _():
            send_out(2)

        @at(13)
        def _():
            send_out(1)

    def turn(t, carry):
        events(t)
        i = 2 * t + 1
        scores(i + 1, s_a)
        soften(i, s_b, p_b, f_b)
        gather(i - 1, p_a, f_a)
        scores(i + 2, s_b)
        soften(i + 1, s_a, p_a, f_a)
        gather(i, p_b, f_b)
        return carry

    lax.fori_loop(1, 15, turn, 0)
    soften(31, s_b, p_b, f_b)
    gather(30, p_a, f_a)
    gather(31, p_b, f_b)
    send_out(0)

    for make, which in sent[2]:
        make(*which).wait_send()
    for core in range(2):
        @pl.when(c == core)
        def _():
            for make, which in sent[core]:
                make(*which).wait_send()
    for k in range(4):
        for other in range(2):
            if k or other:
                o_wait(k, other)

    sub = lax.broadcasted_iota(jnp.int32, (16, HD), 0)
    totals = jnp.zeros((16, HD), jnp.float32)
    for other in range(2):
        half = c if other == 0 else 1 - c
        parts = [ob.at[0, 0] if k == 0 and other == 0 else rb.at[k, other] for k in range(4)]
        logs = [part_ref[HALF:OMSG, :].astype(jnp.float32) for part_ref in parts]
        shares = jnp.zeros((16, HD), jnp.float32)
        for h in range(4):
            log = [v[3 * h:3 * h + 1, :] + v[3 * h + 1:3 * h + 2, :] + v[3 * h + 2:3 * h + 3, :] for v in logs]
            most = jnp.maximum(jnp.maximum(log[0], log[1]), jnp.maximum(log[2], log[3]))
            share = [jnp.exp(v - most) for v in log]
            whole = share[0] + share[1] + share[2] + share[3]
            for k in range(4):
                shares = jnp.where(sub == 4 * h + k, share[k] / whole, shares)
            totals = jnp.where(sub == half * 4 + h, most + jnp.log(whole), totals)
        shares = jnp.concatenate([shares, jnp.zeros((HD - 16, HD), jnp.float32)], axis=0).T
        for h in range(4):
            mixed = jnp.zeros((TOK, HD), jnp.float32)
            for k in range(4):
                share = shares[0:TOK, 4 * h + k:4 * h + k + 1]
                mixed += share * parts[k][h * TOK:(h + 1) * TOK, :].astype(jnp.float32)
            att_ref[:, pl.ds(pl.multiple_of((half * 4 + h) * HD, HD), HD)] = mixed
    lt_ref[...] = totals[0:8, 0:TOK]


def local(queries, keys, values, block_start):
    vmem = pl.BlockSpec(memory_space=pltpu.VMEM)
    hbm = pl.BlockSpec(memory_space=pl.ANY)
    dma = pltpu.SemaphoreType.DMA
    bf16, f32 = jnp.bfloat16, jnp.float32
    attended, log_total = pl.pallas_call(
        kernel,
        out_shape=(
            jax.ShapeDtypeStruct((TOK, 8 * HD), f32),
            jax.ShapeDtypeStruct((8, TOK), f32),
        ),
        in_specs=[pl.BlockSpec(memory_space=pltpu.SMEM), hbm, hbm, hbm],
        out_specs=(vmem, vmem),
        scratch_shapes=[
            pltpu.VMEM((TOK, 8 * HD), bf16),
            pltpu.VMEM((8, 8, MSG, HD), bf16),
            pltpu.VMEM((4, 2, QMSG, HD), bf16),
            pltpu.VMEM((QMSG, HD), bf16),
            pltpu.VMEM((4, 2, OMSG, HD), bf16),
            pltpu.VMEM((4, 2, OMSG, HD), bf16),
            pltpu.VMEM((4, ROWS, 2 * HD), f32),
            pltpu.VMEM((4, ROWS, HD), f32),
            pltpu.VMEM((KEYS, HD), bf16),
            pltpu.VMEM((HALF, HD), bf16),
            pltpu.VMEM((ROWS, KEYS), f32),
            pltpu.VMEM((ROWS, KEYS), f32),
            pltpu.VMEM((ROWS, KEYS), bf16),
            pltpu.VMEM((ROWS, KEYS), bf16),
            pltpu.VMEM((ROWS, HD), f32),
            pltpu.VMEM((ROWS, HD), f32),
            dma((4,)), dma((4,)), dma((8,)), dma((8,)), dma((8, 2)), dma((8, 2)),
            dma((4, 2)), dma((4, 2)), dma((8, 2)), dma((4, 2)),
            dma((4, 2)), dma((4, 2)), dma((4, 2)), dma((4, 2)), dma((3,)),
        ],
        compiler_params=pltpu.CompilerParams(
            collective_id=0, has_side_effects=True, vmem_limit_bytes=48 << 20
        ),
    )(block_start, queries, keys, values)
    return attended, log_total.T


def solution(mesh):
    placed = (
        P(("row", "col"), None),
        P(("row", "col"), None),
        P(("row", "col"), None),
        P(("row", "col")),
    )
    return jax.shard_map(
        local,
        mesh=mesh,
        in_specs=placed,
        out_specs=(P(("row", "col"), None), P(("row", "col"), None)),
        check_vma=False,
    )
```

```python
import functools
import math

import jax
import jax.numpy as jnp
from jax import lax
from jax.experimental import pallas as pl
from jax.experimental.pallas import tpu as pltpu
from jax.sharding import PartitionSpec as P

MESH = pl.DeviceIdType.MESH
TOK = 96
HD = 128
HALF = 4 * TOK
MSG = 2 * TOK + 16
QMSG = HALF + 16
OMSG = HALF + 16
ROWS = 2 * HALF
KEYS = 8 * TOK
REL = (0, 1, 3, 2)
INV = (0, 2, 1, 3)
Z_OFF = (0, 1, 7, 2, 6, 3, 5, 4)
Z_INV = (0, 2, 1, 4, 3, 6, 5, 7)
PLANE_AT = ((0, 0), (1, 4), (2, 0), (2, 4), (5, 0), (5, 4), (7, 0), (7, 4))
Z_AT = ((1, 0), (0, 4), (0, 5), (0, 6), (0, 7), (1, 1), (1, 2), (1, 3))
LINE_AT = (None, 3, 4, 6)
SCALE = HD ** -0.5
C2 = SCALE * math.log2(math.e)
MASKED = -1e30
FLOOR = -1e20


def kernel(start_ref, q_hbm, k_hbm, v_hbm, att_ref, lt_ref, q_ref, kv, qb, qother, ob, rb, acc, peak,
           marks, triangle, s_a, s_b, p_a, p_b, f_a, f_b,
           y_s, y_r, z_s, z_r, a_s, a_r, b_s, b_r, ah_s, bh_s, q_s, q_r, o_s, o_r, in_s):
    row = lax.axis_index("row")
    col = lax.axis_index("col")
    x = lax.rem(row, 4)
    y = lax.div(col, 16) * 2 + lax.div(row, 4)
    z = lax.rem(lax.div(col, 2), 8)
    c = lax.rem(col, 2)

    def device(xx, yy, zz, cc):
        return (lax.rem(yy, 2) * 4 + xx, (lax.div(yy, 2) * 8 + zz) * 2 + cc)

    partner = device(x, y, z, 1 - c)
    y_peer = [None] + [device(x, lax.rem(y + REL[k], 4), z, c) for k in (1, 2, 3)]
    z_up = device(x, y, lax.rem(z + 1, 8), c)
    z_down = device(x, y, lax.rem(z + 7, 8), c)
    z_peer = [device(x, y, lax.rem(z + step, 8), c) for step in Z_OFF]
    x_peer = [[None, partner]] + [
        [device(lax.rem(x + REL[k], 4), y, z, c), device(lax.rem(x + REL[k], 4), y, z, 1 - c)]
        for k in (1, 2, 3)
    ]

    barrier = pltpu.get_barrier_semaphore()

    def greet(peers):
        for peer in peers:
            pl.semaphore_signal(barrier, inc=1, device_id=peer, device_id_type=MESH)

    greet([partner, z_up, z_down, y_peer[1], y_peer[2]] + x_peer[1] + x_peer[2] + x_peer[3])

    @pl.when(c == 0)
    def _():
        greet([y_peer[3]])

    @pl.when(c == 1)
    def _():
        greet(z_peer[3:])

    loads = [
        pltpu.make_async_copy(k_hbm, kv.at[c, 0, pl.ds(0, TOK)], in_s.at[0]),
        pltpu.make_async_copy(v_hbm, kv.at[c, 0, pl.ds(TOK, TOK)], in_s.at[1]),
        pltpu.make_async_copy(q_hbm, q_ref, in_s.at[2]),
    ]
    for load in loads:
        load.start()

    number = jnp.full((16, HD), start_ref[0].astype(jnp.float32), jnp.float32).astype(jnp.bfloat16)
    kv[c, 0, 2 * TOK:MSG, :] = number
    for load in loads[:2]:
        load.wait()

    def copy(src, dst, send, recv, to):
        return pltpu.make_async_remote_copy(
            src_ref=src, dst_ref=dst, send_sem=send, recv_sem=recv, device_id=to, device_id_type=MESH
        )

    sent = ([], [], [])

    def start(make, *which, on=2):
        make(*which).start()
        sent[on].append((make, which))

    def wait(dst, recv):
        copy(dst, dst, recv, recv, partner).wait_recv()

    def q_copy(k, other):
        if other:
            return copy(qother, qb.at[INV[k], 1], q_s.at[k, 1], q_r.at[INV[k], 1], x_peer[k][1])
        return copy(qb.at[0, 0], qb.at[INV[k], 0], q_s.at[k, 0], q_r.at[INV[k], 0], x_peer[k][0])

    def q_wait(k, other):
        copy(qb.at[k, other], qb.at[k, other], q_s.at[k, other], q_r.at[k, other], partner).wait_recv()

    def plane(k, g):
        unit, first = PLANE_AT[k]
        return kv.at[unit, pl.ds(first + 2 * g, 2)]

    def y_copy(k):
        return copy(kv.at[0, 0], kv.at[0, INV[k]], y_s.at[k], y_r.at[INV[k]], y_peer[k])

    def a_copy(k, g):
        if k == 7:
            return copy(plane(5 + g, g), plane(7, g), a_s.at[7, g], a_r.at[7, g], z_down if g else z_up)
        to = z_up if k % 2 == 1 else z_down
        return copy(plane(max(k - 2, 0), g), plane(k, g), a_s.at[k, g], a_r.at[k, g], to)

    def a_hand(k, g):
        return copy(plane(k, g), plane(k, g), ah_s.at[k, g], a_r.at[k, g], partner)

    def pass_a(k, g):
        wait(plane(k, g), a_r.at[k, g])
        if k <= 4:
            start(a_copy, k + 2, g, on=0)
        elif k == 5 + g:
            start(a_copy, 7, g, on=0)
        start(a_hand, k, g, on=0)

    def have_a(*planes):
        @pl.when(c == 1)
        def _():
            for k in planes:
                for g in range(2):
                    wait(plane(k, g), a_r.at[k, g])

    def line(k, g):
        if k == 0:
            return kv.at[g, pl.ds(4 - 4 * g, 4)]
        return kv.at[LINE_AT[k], pl.ds(4 * g, 4)]

    def z_copy(k):
        return copy(kv.at[1, 0], kv.at[Z_AT[Z_INV[k]]], z_s.at[k], z_r.at[Z_INV[k]], z_peer[k])

    def b_copy(k, g):
        if k == 3:
            return copy(line(1 + g, g), line(3, g), b_s.at[3, g], b_r.at[3, g], y_peer[1] if g else y_peer[2])
        return copy(line(0, g), line(INV[k], g), b_s.at[k, g], b_r.at[INV[k], g], y_peer[k])

    def b_hand(k, g):
        return copy(line(k, g), line(k, g), bh_s.at[k, g], b_r.at[k, g], partner)

    def pass_b(k, g):
        wait(line(k, g), b_r.at[k, g])
        if k == 1 + g:
            start(b_copy, 3, g, on=1)
        start(b_hand, k, g, on=1)

    def have_b(k, parts=(0, 1)):
        @pl.when(c == 0)
        def _():
            for g in parts:
                wait(line(k, g), b_r.at[k, g])

    def o_copy(k, other):
        return copy(ob.at[k, other], rb.at[INV[k], other], o_s.at[k, other], o_r.at[INV[k], other], x_peer[k][other])

    def o_wait(k, other):
        copy(rb.at[k, other], rb.at[k, other], o_s.at[k, other], o_r.at[k, other], partner).wait_recv()

    def unit(u):
        if isinstance(u, int):
            if u < 8:
                return u % 4, u // 4
            if u < 14:
                return (u + 1) % 3 + 1, (u + 1) // 3 - 1
            if u < 26:
                return 7 - (u + 2) // 4, 4 + (u + 2) % 4
            return 0, u - 24
        from8, from14, from26 = (lax.div(u + 32 - n, 32) for n in (8, 14, 26))
        query = (
            (1 - from8) * lax.rem(u, 4)
            + (from8 - from14) * (lax.rem(u + 1, 3) + 1) + (from14 - from26) * (7 - lax.div(u + 2, 4))
        )
        slot = (
            (1 - from8) * lax.div(u, 4)
            + (from8 - from14) * (lax.div(u + 1, 3) - 1) + (from14 - from26) * (4 + lax.rem(u + 2, 4)) + from26 * (u - 24)
        )
        return query, slot

    lane = lax.broadcasted_iota(jnp.int32, (1, HD), 1)
    ones = jnp.ones((KEYS, HD), jnp.bfloat16)

    def number_of(ref):
        return ref[...].astype(jnp.float32)[0:1, :]

    def scores(u, s):
        query, slot = unit(u)
        numbers = [number_of(kv.at[slot, i, pl.ds(2 * TOK, 16)]) for i in range(8)]
        rows = []
        for half in range(2):
            mine = number_of(qb.at[query, half, pl.ds(HALF, 16)])
            hidden = jnp.zeros((1, HD), jnp.float32)
            for i in range(8):
                hidden = jnp.where((lane == i) & (numbers[i] > mine), MASKED, hidden)
            same = jnp.where(numbers[0] == mine, 1.0, 0.0).astype(jnp.bfloat16)
            hidden = triangle[...] * same + hidden.astype(jnp.bfloat16)
            rows.append(jnp.concatenate([qb[query, half, 0:HALF, :], hidden], axis=1))
        rows = jnp.concatenate(rows, axis=0)
        keys = jnp.concatenate([kv[slot, :, 0:TOK, :].reshape(KEYS, HD), marks[...]], axis=1)
        s[...] = lax.dot_general(rows, keys, (((1,), (1,)), ((), ())), preferred_element_type=jnp.float32)

    def soften(u, s, p, f):
        query, slot = unit(u)
        for half in range(2):
            at = pl.ds(half * HALF, HALF)
            v = s[at, :]
            old = peak[query, at, :]
            new = jnp.maximum(old, jnp.max(v, axis=1, keepdims=True))
            p[at, :] = jnp.exp2((v - new[:, :1]) * C2).astype(jnp.bfloat16)
            f[at, :] = jnp.exp2((old - new) * C2)
            peak[query, at, :] = new

    def gather(u, p, f):
        query, slot = unit(u)
        vals = kv[slot, :, TOK:2 * TOK, :].reshape(KEYS, HD)
        vals = jnp.concatenate([vals, ones], axis=1)
        factor = jnp.concatenate([f[...], f[...]], axis=1)
        acc[query] = acc[query] * factor + jnp.dot(p[...], vals, preferred_element_type=jnp.float32)

    def finish(k, half):
        at = pl.ds(half * HALF, HALF)
        total = acc[k, at, HD:2 * HD]
        safe = jnp.where(total > 0.0, total, 1.0)
        ob[k, half, 0:HALF, :] = (acc[k, at, 0:HD] / safe).astype(jnp.bfloat16)
        sums = jnp.ones((TOK, HD), jnp.float32)
        tops = jnp.zeros((TOK, HD), jnp.float32)
        for h in range(4):
            mine = lax.div(lane, 3) == h
            sums = jnp.where(mine, total[h * TOK:(h + 1) * TOK, :], sums)
            tops = jnp.where(mine, peak[k, pl.ds(half * HALF + h * TOK, TOK), :], tops)
        some = sums > 0.0
        log = jnp.where(some, tops * SCALE + jnp.log(jnp.where(some, sums, 1.0)), MASKED)
        hi = log.astype(jnp.bfloat16).astype(jnp.float32)
        mid = (log - hi).astype(jnp.bfloat16).astype(jnp.float32)
        turn_of = lax.rem(lane, 3)
        packed = jnp.where(turn_of == 0, hi, jnp.where(turn_of == 1, mid, log - hi - mid))
        packed = jnp.concatenate([packed, jnp.zeros((HD - TOK, HD), jnp.float32)], axis=0)
        ob[k, half, HALF:OMSG, :] = packed.T[0:16, :].astype(jnp.bfloat16)

    def send_out(k):
        for half in (1, 0):
            finish(k, half)
            if k or half:
                start(o_copy, k, half)

    pl.semaphore_wait(barrier, 12 + 4 * c)

    @pl.when(c == 0)
    def _():
        for k in (1, 2, 3):
            start(y_copy, k, on=0)

    @pl.when(c == 1)
    def _():
        for k in range(1, 8):
            start(z_copy, k, on=1)

    loads[2].wait()
    for h in range(4):
        here = pl.ds(pl.multiple_of((c * 4 + h) * HD, HD), HD)
        there = pl.ds(pl.multiple_of(((1 - c) * 4 + h) * HD, HD), HD)
        qb[0, 0, h * TOK:(h + 1) * TOK, :] = q_ref[:, here]
        qother[h * TOK:(h + 1) * TOK, :] = q_ref[:, there]
    qb[0, 0, HALF:QMSG, :] = number
    qother[HALF:QMSG, :] = number
    start(q_copy, 0, 1)
    for k in (1, 2):
        for other in range(2):
            start(q_copy, k, other)

    acc[...] = jnp.zeros_like(acc)
    peak[...] = jnp.full(peak.shape, FLOOR, jnp.float32)
    key = lax.broadcasted_iota(jnp.int32, (KEYS, HD), 0)
    mark = lax.broadcasted_iota(jnp.int32, (KEYS, HD), 1)
    marked = (lax.div(key, TOK) == mark) & (mark < 8) | (key + 8 == mark) & (key < TOK)
    marks[...] = jnp.where(marked, 1.0, 0.0).astype(jnp.bfloat16)
    token = lax.rem(lax.broadcasted_iota(jnp.int32, (HALF, HD), 0), TOK)
    later = lax.broadcasted_iota(jnp.int32, (HALF, HD), 1) - 8 > token
    triangle[...] = jnp.where(later, MASKED, 0.0).astype(jnp.bfloat16)

    @pl.when(c == 0)
    def _():
        wait(kv.at[0, 1], y_r.at[1])
        start(a_copy, 1, 0, on=0)
        start(a_copy, 2, 0, on=0)
        start(a_hand, 0, 0, on=0)
        wait(kv.at[0, 2], y_r.at[2])
        wait(kv.at[0, 3], y_r.at[3])
        start(a_copy, 1, 1, on=0)
        start(a_copy, 2, 1, on=0)
        start(a_hand, 0, 1, on=0)

    def line_done(g):
        for k in (range(5, 8) if g else range(1, 5)):
            wait(kv.at[Z_AT[k]], z_r.at[k])
        start(b_copy, 1, g, on=1)
        start(b_copy, 2, g, on=1)
        start(b_hand, 0, g, on=1)

    @pl.when(c == 1)
    def _():
        line_done(0)

    for other in range(2):
        start(q_copy, 3, other)
    have_a(0)
    have_b(0, (0,))
    q_wait(0, 1)
    scores(0, s_a)
    soften(0, s_a, p_a, f_a)
    q_wait(1, 0)
    q_wait(1, 1)
    scores(1, s_b)
    q_wait(2, 0)
    q_wait(2, 1)
    scores(2, s_a)
    soften(1, s_b, p_b, f_b)
    gather(0, p_a, f_a)

    @pl.when(c == 0)
    def _():
        for g in range(2):
            for k in (1, 2):
                pass_a(k, g)

    @pl.when(c == 1)
    def _():
        line_done(1)

    q_wait(3, 0)
    q_wait(3, 1)
    scores(3, s_b)
    soften(2, s_a, p_a, f_a)
    gather(1, p_b, f_b)

    def events(t):
        def at(step, core=None):
            return pl.when(t == step) if core is None else pl.when((t == step) & (c == core))

        @at(1)
        def _():
            have_a(1)
            have_b(0, (1,))

        @at(2, 0)
        def _():
            for g in range(2):
                for k in (3, 4):
                    pass_a(k, g)

        @at(3, 1)
        def _():
            for g in range(2):
                for k in (1, 2):
                    pass_b(k, g)

        @at(4, 0)
        def _():
            for g in range(2):
                for k in (5, 6):
                    pass_a(k, g)

        @at(3)
        def _():
            have_a(2, 3)

        @at(4)
        def _():
            have_b(1)

        @at(5, 1)
        def _():
            for g in range(2):
                pass_b(3, g)

        @at(6, 0)
        def _():
            for g in range(2):
                pass_a(7, g)

        @at(6)
        def _():
            have_b(2)
            have_a(4, 5)

        @at(7)
        def _():
            have_b(3)
            have_a(6, 7)

        @at(9)
        def _():
            send_out(3)

        @at(11)
        def _():
            send_out(2)

        @at(13)
        def _():
            send_out(1)

    def turn(t, carry):
        events(t)
        i = 2 * t + 1
        scores(i + 1, s_a)
        soften(i, s_b, p_b, f_b)
        gather(i - 1, p_a, f_a)
        scores(i + 2, s_b)
        soften(i + 1, s_a, p_a, f_a)
        gather(i, p_b, f_b)
        return carry

    lax.fori_loop(1, 15, turn, 0)
    soften(31, s_b, p_b, f_b)
    gather(30, p_a, f_a)
    gather(31, p_b, f_b)
    send_out(0)

    for make, which in sent[2][:-1]:
        make(*which).wait_send()
    for core in range(2):
        @pl.when(c == core)
        def _():
            for make, which in sent[core]:
                make(*which).wait_send()

    sub = lax.broadcasted_iota(jnp.int32, (16, HD), 0)
    totals = jnp.zeros((16, HD), jnp.float32)
    for other in range(2):
        for k in range(4):
            if k or other:
                o_wait(k, other)
        half = c if other == 0 else 1 - c
        parts = [ob.at[0, 0] if k == 0 and other == 0 else rb.at[k, other] for k in range(4)]
        logs = [part_ref[HALF:OMSG, :].astype(jnp.float32) for part_ref in parts]
        shares = jnp.zeros((16, HD), jnp.float32)
        for h in range(4):
            log = [v[3 * h:3 * h + 1, :] + v[3 * h + 1:3 * h + 2, :] + v[3 * h + 2:3 * h + 3, :] for v in logs]
            most = jnp.maximum(jnp.maximum(log[0], log[1]), jnp.maximum(log[2], log[3]))
            share = [jnp.exp(v - most) for v in log]
            whole = share[0] + share[1] + share[2] + share[3]
            for k in range(4):
                shares = jnp.where(sub == 4 * h + k, share[k] / whole, shares)
            totals = jnp.where(sub == half * 4 + h, most + jnp.log(whole), totals)
        shares = jnp.concatenate([shares, jnp.zeros((HD - 16, HD), jnp.float32)], axis=0).T
        for h in range(4):
            mixed = jnp.zeros((TOK, HD), jnp.float32)
            for k in range(4):
                share = shares[0:TOK, 4 * h + k:4 * h + k + 1]
                mixed += share * parts[k][h * TOK:(h + 1) * TOK, :].astype(jnp.float32)
            att_ref[:, pl.ds(pl.multiple_of((half * 4 + h) * HD, HD), HD)] = mixed
    lt_ref[...] = totals[0:8, 0:TOK]
    make, which = sent[2][-1]
    make(*which).wait_send()


def local(queries, keys, values, block_start):
    vmem = pl.BlockSpec(memory_space=pltpu.VMEM)
    hbm = pl.BlockSpec(memory_space=pl.ANY)
    dma = pltpu.SemaphoreType.DMA
    bf16, f32 = jnp.bfloat16, jnp.float32
    attended, log_total = pl.pallas_call(
        kernel,
        out_shape=(
            jax.ShapeDtypeStruct((TOK, 8 * HD), f32),
            jax.ShapeDtypeStruct((8, TOK), f32),
        ),
        in_specs=[pl.BlockSpec(memory_space=pltpu.SMEM), hbm, hbm, hbm],
        out_specs=(vmem, vmem),
        scratch_shapes=[
            pltpu.VMEM((TOK, 8 * HD), bf16),
            pltpu.VMEM((8, 8, MSG, HD), bf16),
            pltpu.VMEM((4, 2, QMSG, HD), bf16),
            pltpu.VMEM((QMSG, HD), bf16),
            pltpu.VMEM((4, 2, OMSG, HD), bf16),
            pltpu.VMEM((4, 2, OMSG, HD), bf16),
            pltpu.VMEM((4, ROWS, 2 * HD), f32),
            pltpu.VMEM((4, ROWS, HD), f32),
            pltpu.VMEM((KEYS, HD), bf16),
            pltpu.VMEM((HALF, HD), bf16),
            pltpu.VMEM((ROWS, KEYS), f32),
            pltpu.VMEM((ROWS, KEYS), f32),
            pltpu.VMEM((ROWS, KEYS), bf16),
            pltpu.VMEM((ROWS, KEYS), bf16),
            pltpu.VMEM((ROWS, HD), f32),
            pltpu.VMEM((ROWS, HD), f32),
            dma((4,)), dma((4,)), dma((8,)), dma((8,)), dma((8, 2)), dma((8, 2)),
            dma((4, 2)), dma((4, 2)), dma((8, 2)), dma((4, 2)),
            dma((4, 2)), dma((4, 2)), dma((4, 2)), dma((4, 2)), dma((3,)),
        ],
        compiler_params=pltpu.CompilerParams(
            collective_id=0, has_side_effects=True, vmem_limit_bytes=48 << 20
        ),
    )(block_start, queries, keys, values)
    return attended, log_total.T


def solution(mesh):
    placed = (
        P(("row", "col"), None),
        P(("row", "col"), None),
        P(("row", "col"), None),
        P(("row", "col")),
    )
    return jax.shard_map(
        local,
        mesh=mesh,
        in_specs=placed,
        out_specs=(P(("row", "col"), None), P(("row", "col"), None)),
        check_vma=False,
    )
```
